32 devices in a mesh: groups: 2 (over y), gx: 16 (over z, x, core).
Axes of the slice: x: 2, y: 2, z: 4, core: 2. Of those that a mesh axis runs over, the one named last changes fastest.
Arguments:
- grad_out: bfloat16 [64, 4, 128, 128], P(('groups', 'gx')), parts along dimension 0, may hold values from -6 to 6
- inputs: bfloat16 [64, 4, 128, 128], P(('groups', 'gx')), parts along dimension 0, may hold values from -6 to 6
- pre_first: bfloat16 [64, 4, 128, 128], P(('groups', 'gx')), parts along dimension 0, may hold values from -6 to 6
- pre_second: bfloat16 [64, 4, 128, 128], P(('groups', 'gx')), parts along dimension 0, may hold values from -6 to 6
- filter_first: bfloat16 [3456, 128], P('gx'), may hold values from -0.109375 to 0.109375
- filter_second: bfloat16 [3456, 128], P('gx'), may hold values from -0.109375 to 0.109375
Outputs:
- grad_inputs: bfloat16 [64, 4, 128, 128], P(('groups', 'gx')), parts along dimension 0
- grad_filter_first: float32 [3456, 256], P('gx', 'groups'), parts along dimension 1
- grad_filter_second: float32 [3456, 256], P('gx', 'groups'), parts along dimension 1
The draws below stay inside these ranges and needn't reach their ends.
There are 2 independent parts, one for each index of `groups`. The reference program is written for one: setup_inputs(seed, part) draws one part's arguments, and reference() takes and returns one part's arrays. A program takes and returns all parts, laid end to end along the dimension named above; an argument that names none is the same for every part. Nothing has to cross between parts.
All inputs are finite; a program needn't handle non-finite values.
Results may differ from the reference program's by a relative error of at most 0.0058.
Values may be sent and summed in bfloat16 or wider, within the bound.
No kernel may reach another device: no remote copies, remote signals or barrier semaphores. Data moves between devices by JAX's collectives and lax.ppermute only.
A program may use at most 64 MiB of HBM per device.

```python
import math
import jax
import jax.numpy as jnp
from jax import lax

C = 128
Y = 4
Z = 128
NX = 32


def level_of(key, dims, pieces, least, largest):
    level, own = 1.0, jax.random.fold_in(key, 6)
    for position, parts in pieces:
        heights = jnp.exp(jax.random.uniform(jax.random.fold_in(own, position), (parts,), jnp.float32, least / len(pieces), largest / len(pieces)))
        level = level * jnp.repeat(heights, dims[position] // parts).reshape([-1 if axis == position else 1 for axis in range(len(dims))])
    return level


def noise(key, dims, width, most, split=(), dtype=jnp.bfloat16):
    entries = width * jax.random.normal(key, dims, jnp.float32)
    if split:
        entries = entries * level_of(key, dims, split, -0.22, 0.18)
    return jnp.clip(entries, -most, most).astype(dtype)


def setup_inputs(seed: int = 0, part: int = 0) -> dict:
    key_of = jax.random.split(jax.random.key(seed), 7)
    part_splits = jax.random.split(jax.random.fold_in(key_of[6], part), 7)
    return {
        "grad_out": noise(part_splits[0], (NX, Y, Z, C), 1.0, 6.0, ((0, 16),)),
        "inputs": noise(part_splits[1], (NX, Y, Z, C), 1.0, 6.0, ((0, 16),)),
        "pre_first": noise(part_splits[2], (NX, Y, Z, C), 1.0, 6.0, ((0, 16),)),
        "pre_second": noise(part_splits[3], (NX, Y, Z, C), 1.0, 6.0, ((0, 16),)),
        "filter_first": noise(key_of[4], (27 * C, C), (27 * C) ** -0.5, 0.109375, ((0, 16),)),
        "filter_second": noise(key_of[5], (27 * C, C), (27 * C) ** -0.5, 0.109375, ((0, 16),)),
    }


inv_root_two = 0.7071067811865476
inv_root_twopi = 0.3989422804014327

def gelu_parts(value):
    normal_cdf = 0.5 * (1.0 + lax.erf(value * inv_root_two))
    return (value * normal_cdf, normal_cdf + value * jnp.exp(-0.5 * value * value) * inv_root_twopi)

def pad_field(field):
    return jnp.pad(field, ((1, 1), (1, 1), (1, 1), (0, 0)))

def back_data(grads, weights):
    x_cells, y_cells, z_cells, channels = grads.shape
    padded = pad_field(grads.astype(jnp.float32))
    weights = weights.astype(jnp.float32)
    running = jnp.zeros((x_cells * y_cells * z_cells, channels), jnp.float32)
    for shift_a in (-1, 0, 1):
        for shift_b in (-1, 0, 1):
            for shift_c in (-1, 0, 1):
                index = 9 * (shift_a + 1) + 3 * (shift_b + 1) + (shift_c + 1)
                tap = weights[index * channels:(index + 1) * channels]
                piece = padded[1 - shift_a:1 - shift_a + x_cells, 1 - shift_b:1 - shift_b + y_cells, 1 - shift_c:1 - shift_c + z_cells].reshape(-1, channels)
                running = running + jnp.dot(piece, tap.T, precision=lax.Precision.HIGHEST)
    return running.reshape(grads.shape)

def back_filter(saved, grads):
    x_cells, y_cells, z_cells, channels = grads.shape
    padded = pad_field(saved.astype(jnp.float32))
    flat_grads = grads.astype(jnp.float32).reshape(-1, channels)
    blocks = []
    for shift_a in (-1, 0, 1):
        for shift_b in (-1, 0, 1):
            for shift_c in (-1, 0, 1):
                piece = padded[1 + shift_a:1 + shift_a + x_cells, 1 + shift_b:1 + shift_b + y_cells, 1 + shift_c:1 + shift_c + z_cells].reshape(-1, channels)
                blocks.append(jnp.dot(piece.T, flat_grads, precision=lax.Precision.HIGHEST))
    return jnp.concatenate(blocks, axis=0)

def reference(grad_out, inputs, pre_first, pre_second, filter_first, filter_second):
    grad_scale = 1.0 / math.sqrt(NX * Y * Z)
    unused_value, slope_two = gelu_parts(pre_second.astype(jnp.float32))
    grad_two = (grad_out.astype(jnp.float32) * slope_two).astype(jnp.bfloat16)
    act_one, slope_one = gelu_parts(pre_first.astype(jnp.float32))
    act_one = act_one.astype(jnp.bfloat16)
    grad_act = back_data(grad_two, filter_second)
    filt_two = back_filter(act_one, grad_two)
    grad_one = (grad_act * slope_one).astype(jnp.bfloat16)
    grad_in = back_data(grad_one, filter_first)
    filt_one = back_filter(inputs, grad_one)
    return (grad_in.astype(jnp.bfloat16), filt_one * grad_scale, filt_two * grad_scale)
```

```python
import functools
import math

import jax
import jax.numpy as jnp
from jax import lax
from jax.experimental import pallas as pl
from jax.experimental.pallas import tpu as pltpu
from jax.sharding import PartitionSpec as P

inv_root_two = 0.7071067811865476
inv_root_twopi = 0.3989422804014327
shifts = (-1, 0, 1)
planes = tuple((a, b) for a in shifts for b in shifts)
bf16, f32 = jnp.bfloat16, jnp.float32
vmem = pl.BlockSpec(memory_space=pltpu.VMEM)
smem = pl.BlockSpec(memory_space=pltpu.SMEM)
vmem_bytes = 50 * 1024 * 1024


def cdf_of(value):
    return 0.5 * (1.0 + lax.erf(value * inv_root_two))


def slope_of(value):
    return cdf_of(value) + value * jnp.exp(-0.5 * value * value) * inv_root_twopi


def value_of(value):
    return value * cdf_of(value)


def shift_rows(block, c):
    rows = block.shape[0]
    if c == 0:
        return block
    place = lax.broadcasted_iota(jnp.int32, block.shape, 0)
    edge = 0 if c == 1 else rows - 1
    return jnp.where(place == edge, 0.0, pltpu.roll(block, c % rows, 0))


def zero_sides(ref):
    layers, wide = ref.shape[:2]
    blank = jnp.zeros(ref.shape[2:], ref.dtype)
    for x in range(layers):
        ref[x, 0] = blank
        ref[x, wide - 1] = blank


def first_grads(grad_out, pre_second, pre_first, own, up, down):
    nx = own.shape[0]
    for x in range(nx):
        for y in range(own.shape[1]):
            slope = slope_of(pre_second[x, y].astype(f32))
            own[x, y] = (grad_out[x, y].astype(f32) * slope).astype(bf16)
    up[0:2] = own[nx - 2 : nx]
    up[2:3] = pre_first[nx - 1 : nx]
    down[0:2] = own[0:2]
    down[2:3] = pre_first[0:1]


def filter_terms(load, padded, first, turned, total, scale):
    nx, ny = padded.shape[0] - 2 * first, padded.shape[1] - 2
    nz, ch = padded.shape[2:]
    for x in range(nx):
        for y in range(ny):
            block = load(x, y)
            for k, c in enumerate(shifts):
                at = (x * ny + y) * nz
                moved = shift_rows(block, -c).astype(bf16)
                turned[k * ch : (k + 1) * ch, at : at + nz] = moved.T
    rows = nx * ny * nz

    def piece(a, b):
        return padded[first - a : first - a + nx, 1 - b : 1 - b + ny].reshape(rows, ch)

    for i in range(0, len(planes), 2):
        pair = planes[i : i + 2]
        right = jnp.concatenate([piece(a, b) for a, b in pair], axis=1)
        part = jnp.dot(turned[...], right, preferred_element_type=f32) * scale
        for j in range(len(pair)):
            total[(i + j) * 3 * ch : (i + j + 1) * 3 * ch] = part[:, j * ch : (j + 1) * ch]


def data_layers(padded, first, weights, finish, out_x):
    ny = padded.shape[1] - 2
    nz, ch = padded.shape[2:]
    rows = ny * nz
    for x in out_x:
        total = None
        for i in range(0, len(planes), 2):
            pair = planes[i : i + 2]
            left = jnp.concatenate(
                [padded[first + x - a, 1 - b : 1 - b + ny].reshape(rows, ch) for a, b in pair], axis=1
            )
            right = jnp.concatenate(
                [weights[(i + j) * 3 * ch : (i + j + 1) * 3 * ch] for j in range(len(pair))], axis=1
            )
            part = lax.dot_general(left, right, (((1,), (1,)), ((), ())), preferred_element_type=f32)
            total = part if total is None else total + part
        for y in range(ny):
            block = total[y * nz : (y + 1) * nz]
            value = sum(shift_rows(block[:, k * ch : (k + 1) * ch], c) for k, c in enumerate(shifts))
            finish(x, y, value)


def split_halves(total, which, kept, sent):
    half, rows = kept.shape[:2]
    for k in range(half):
        kept[k] = total[pl.ds(pl.multiple_of((2 * k + which) * rows, 8), rows)]
        sent[k] = total[pl.ds(pl.multiple_of((2 * k + 1 - which) * rows, 8), rows)].astype(bf16)


def second_filter(spot, pre_first, own, low, high, kept, sent, padded, turned, total, *, scale):
    nx, ny = own.shape[:2]
    zero_sides(padded)
    padded[0, 1 : 1 + ny] = low[1]
    padded[1 : 1 + nx, 1 : 1 + ny] = own[...]
    padded[1 + nx, 1 : 1 + ny] = high[0]

    def load(x, y):
        return value_of(pre_first[x, y].astype(f32)).astype(bf16).astype(f32)

    filter_terms(load, padded, 1, turned, total, scale)
    split_halves(total, lax.rem(spot[0], 2), kept, sent)


def first_filter(spot, pre_first, inputs, own, low, high, weights, kept, sent, wide, padded, turned, total, *, scale):
    nx, ny = own.shape[:2]
    zero_sides(padded)
    padded[0:2, 1 : 1 + ny] = low[0:2]
    padded[2 : 2 + nx, 1 : 1 + ny] = own[...]
    padded[2 + nx : 4 + nx, 1 : 1 + ny] = high[0:2]
    zero_sides(wide)

    def finish(x, y, value):
        if x < 0:
            slope = slope_of(low[2, y].astype(f32))
            value = jnp.where(spot[0] > 0, value * slope, 0.0)
        elif x == nx:
            slope = slope_of(high[2, y].astype(f32))
            value = jnp.where(spot[0] < spot[1] - 1, value * slope, 0.0)
        else:
            value = value * slope_of(pre_first[x, y].astype(f32))
        wide[1 + x, 1 + y] = value.astype(bf16)

    data_layers(padded, 2, weights, finish, range(-1, nx + 1))

    def load(x, y):
        return inputs[x, y].astype(f32)

    filter_terms(load, wide, 1, turned, total, scale)
    split_halves(total, lax.rem(spot[0], 2), kept, sent)


def input_grads(wide, weights, out):
    def finish(x, y, value):
        out[x, y] = value.astype(bf16)

    data_layers(wide, 1, weights, finish, range(out.shape[0]))


def call(body, n_smem, args, outs, scratch=()):
    return pl.pallas_call(
        body,
        in_specs=[smem] * n_smem + [vmem] * (len(args) - n_smem),
        out_specs=[vmem] * len(outs),
        out_shape=[jax.ShapeDtypeStruct(s, d) for s, d in outs],
        scratch_shapes=[pltpu.VMEM(s, d) for s, d in scratch],
        compiler_params=pltpu.CompilerParams(vmem_limit_bytes=vmem_bytes),
    )(*args)


def on_device(grad_out, inputs, pre_first, pre_second, filter_first, filter_second):
    shape = grad_out.shape
    nx, ny, nz, ch = shape
    n = lax.axis_size("gx")
    me = lax.axis_index("gx")
    bits = [1 << k for k in range(n.bit_length() - 1)]
    rows = filter_first.shape[0]
    scale = 1.0 / math.sqrt(nx * n * ny * nz)
    spot = jnp.stack([me, jnp.full((), n, me.dtype)]).astype(jnp.int32)

    def swap(array, bit):
        return lax.ppermute(array, "gx", [(i, i ^ bit) for i in range(n)])

    full = jnp.stack([filter_first, filter_second])
    for bit in reversed(bits):
        other = swap(full, bit)
        low = (me & bit) == 0
        full = jnp.stack([jnp.where(low, full, other), jnp.where(low, other, full)], axis=-3)
    full = full.reshape(2, n * rows, ch)
    full_first, full_second = full[0], full[1]

    grad_two, up, down = call(
        first_grads, 0, (grad_out, pre_second, pre_first), [(shape, bf16)] + [((3,) + shape[1:], bf16)] * 2
    )
    ahead = [(i, i + 1) for i in range(n - 1)]
    low = lax.ppermute(up, "gx", ahead)
    high = lax.ppermute(down, "gx", [(b, a) for a, b in ahead])

    half = [((n // 2, rows, ch), f32), ((n // 2, rows, ch), bf16)]
    work = [((3 * ch, nx * ny * nz), bf16), ((n * rows, ch), f32)]

    def finish_scatter(kept, sent):
        total = kept + swap(sent, 1).astype(f32)
        for bit in bits[1:]:
            view = total.reshape(-1, 2, rows, ch)
            side = (me & bit) // bit
            mine = lax.dynamic_index_in_dim(view, side, 1, False)
            theirs = lax.dynamic_index_in_dim(view, 1 - side, 1, False)
            total = mine + swap(theirs.astype(bf16), bit).astype(f32)
        return total.reshape(rows, ch)

    kept_two, sent_two = call(
        functools.partial(second_filter, scale=scale),
        1,
        (spot, pre_first, grad_two, low, high),
        half,
        [((nx + 2, ny + 2, nz, ch), bf16)] + work,
    )
    owned_two = finish_scatter(kept_two, sent_two)
    kept_one, sent_one, wide = call(
        functools.partial(first_filter, scale=scale),
        1,
        (spot, pre_first, inputs, grad_two, low, high, full_second),
        half + [((nx + 2, ny + 2, nz, ch), bf16)],
        [((nx + 4, ny + 2, nz, ch), bf16)] + work,
    )
    owned_one = finish_scatter(kept_one, sent_one)
    (grad_in,) = call(input_grads, 0, (wide, full_first), [(shape, bf16)])
    return (grad_in, owned_one, owned_two)


def solution(mesh):
    return jax.shard_map(
        on_device,
        mesh=mesh,
        in_specs=(
            P(("groups", "gx"), None, None, None),
            P(("groups", "gx"), None, None, None),
            P(("groups", "gx"), None, None, None),
            P(("groups", "gx"), None, None, None),
            P("gx", None),
            P("gx", None),
        ),
        out_specs=(P(("groups", "gx"), None, None, None), P("gx", "groups"), P("gx", "groups")),
        check_vma=False,
    )
```

```python
import functools
import math

import jax
import jax.numpy as jnp
from jax import lax
from jax.experimental import pallas as pl
from jax.experimental.pallas import tpu as pltpu
from jax.sharding import PartitionSpec as P

inv_root_two = 0.7071067811865476
inv_root_twopi = 0.3989422804014327
shifts = (-1, 0, 1)
planes = tuple((a, b) for a in shifts for b in shifts)
bf16, f32 = jnp.bfloat16, jnp.float32
vmem = pl.BlockSpec(memory_space=pltpu.VMEM)
smem = pl.BlockSpec(memory_space=pltpu.SMEM)
anywhere = pl.BlockSpec(memory_space=pl.ANY)
vmem_bytes = 14 * 1024 * 1024


def cdf_of(value):
    return 0.5 * (1.0 + lax.erf(value * inv_root_two))


def slope_of(value):
    return cdf_of(value) + value * jnp.exp(-0.5 * value * value) * inv_root_twopi


def value_of(value):
    return value * cdf_of(value)


def shift_rows(block, c):
    rows = block.shape[0]
    if c == 0:
        return block
    place = lax.broadcasted_iota(jnp.int32, block.shape, 0)
    edge = 0 if c == 1 else rows - 1
    return jnp.where(place == edge, 0.0, pltpu.roll(block, c % rows, 0))


def zero_sides(ref):
    layers, wide = ref.shape[:2]
    blank = jnp.zeros(ref.shape[2:], ref.dtype)
    for x in range(layers):
        ref[x, 0] = blank
        ref[x, wide - 1] = blank


def first_grads(spot, grad_out, pre_second, inputs, own, near, far):
    nx = own.shape[0]
    for x in range(nx):
        for y in range(own.shape[1]):
            slope = slope_of(pre_second[x, y].astype(f32))
            own[x, y] = (grad_out[x, y].astype(f32) * slope).astype(bf16)
    send_edges(spot, own, near, far)
    at = near_edge(spot, nx - 1)
    near[1] = inputs[at]
    far[1] = inputs[nx - 1 - at]


def near_edge(spot, last):
    return last * (1 - spot[2])


def send_edges(spot, own, near, far):
    last = own.shape[0] - 1
    at = near_edge(spot, last)
    near[0] = own[at]
    far[0] = own[last - at]


def filter_terms(turned, padded, emit, scale):
    nx, ny = padded.shape[0] - 2, padded.shape[1] - 2
    nz, ch = padded.shape[2:]
    rows = nx * ny * nz

    def piece(a, b):
        return padded[1 - a : 1 - a + nx, 1 - b : 1 - b + ny].reshape(rows, ch)

    for i in range(0, len(planes), 2):
        pair = planes[i : i + 2]
        right = jnp.concatenate([piece(a, b) for a, b in pair], axis=1)
        part = jnp.dot(turned[...], right, preferred_element_type=f32) * scale
        for j in range(len(pair)):
            emit(i + j, part[:, j * ch : (j + 1) * ch])


def prepare(pre_first, inputs, turned, turned_own, slope):
    nx, ny, nz, ch = pre_first.shape
    for x in range(nx):
        for y in range(ny):
            value = pre_first[x, y].astype(f32)
            slope[x, y] = slope_of(value)
            block = value_of(value).astype(bf16).astype(f32)
            at = (x * ny + y) * nz
            for k, c in enumerate(shifts):
                turned[k * ch : (k + 1) * ch, at : at + nz] = shift_rows(block, -c).T.astype(bf16)
            turned_own[x, y] = inputs[x, y].astype(f32).T.astype(bf16)


def stack_turned(stacked, turned_own, turned_sides):
    nx, ny, ch, nz = turned_own.shape
    blank = jnp.zeros((ch, nz), bf16)
    for i, (a, b) in enumerate(planes):
        for x in range(nx):
            for y in range(ny):
                if 0 <= y + b < ny:
                    inside = 0 <= x + a < nx
                    block = turned_own[x + a, y + b] if inside else turned_sides[int(x + a == nx), y + b]
                else:
                    block = blank
                at = (x * ny + y) * nz
                stacked[i * ch : (i + 1) * ch, at : at + nz] = block


def data_layers(padded, weights, finish, out_x):
    ny = padded.shape[1] - 2
    nz, ch = padded.shape[2:]
    rows = ny * nz
    for x in out_x:
        total = None
        for i in range(0, len(planes), 2):
            pair = planes[i : i + 2]
            left = jnp.concatenate(
                [padded[1 + x - a, 1 - b : 1 - b + ny].reshape(rows, ch) for a, b in pair], axis=1
            )
            right = jnp.concatenate([weights(i + j) for j in range(len(pair))], axis=1)
            part = lax.dot_general(left, right, (((1,), (1,)), ((), ())), preferred_element_type=f32)
            total = part if total is None else total + part
        for y in range(ny):
            block = total[y * nz : (y + 1) * nz]
            value = sum(shift_rows(block[:, k * ch : (k + 1) * ch], c) for k, c in enumerate(shifts))
            finish(x, y, value)


def fill_padded(spot, padded, own, near, far):
    nx, ny = own.shape[:2]
    zero_sides(padded)
    padded[1 : 1 + nx, 1 : 1 + ny] = own[...]
    at = near_edge(spot, nx + 1)
    padded[at, 1 : 1 + ny] = near[0]
    padded[nx + 1 - at, 1 : 1 + ny] = far[0]


def split_halves(total, side, kept, sent):
    half, rows = kept.shape[:2]
    for k in range(half):
        kept[k] = total[pl.ds(pl.multiple_of((2 * k + side) * rows, 8), rows)]
        sent[k] = total[pl.ds(pl.multiple_of((2 * k + 1 - side) * rows, 8), rows)].astype(bf16)


def plain_weights(full):
    ch = full.shape[1]
    return lambda plane: full[plane * 3 * ch : (plane + 1) * 3 * ch]


def placed_weights(spot, masks, mine, theirs, pairs):
    even = spot[2] == 0
    for mask, first, second in zip(masks, mine, theirs):
        one, two = first[...].astype(f32), second[...].astype(f32)
        both = jnp.concatenate([jnp.where(even, one, two), jnp.where(even, two, one)], axis=0)
        pairs[lax.bitwise_xor(spot[0] // 2, mask // 2)] = both.astype(bf16)
    wide, ch = pairs.shape[1:]

    def weights(plane):
        at, end = plane * 3 * ch, (plane + 1) * 3 * ch
        pieces = []
        while at < end:
            stop = min(end, (at // wide + 1) * wide)
            pieces.append(pairs[at // wide, at % wide : at % wide + stop - at])
            at = stop
        return jnp.concatenate(pieces, axis=0) if len(pieces) > 1 else pieces[0]

    return weights


def second_filter(spot, own, near, far, turned, *rest, scale, fast):
    total, outs = (rest[-1], rest[:2]) if fast else (rest[0], ())
    turned_sides, padded = rest[2:4] if fast else rest[1:3]
    ny = own.shape[1]
    fill_padded(spot, padded, own, near, far)

    def emit(plane, part):
        ch = part.shape[1]
        total[plane * 3 * ch : (plane + 1) * 3 * ch] = part

    filter_terms(turned, padded, emit, scale)
    if fast:
        split_halves(total, spot[2], *outs)
    high = near_edge(spot, 1)
    for y in range(ny):
        turned_sides[high, y] = near[1, y].astype(f32).T.astype(bf16)
        turned_sides[1 - high, y] = far[1, y].astype(f32).T.astype(bf16)


def both_columns(lists):
    split = [[ref.at[k] for k in range(ref.shape[0])] for ref in lists]
    return split[0] + split[1], split[2] + split[3]


def first_filter(spot, slope, own, near, far, turned_own, turned_sides, *rest, scale, masks):
    nx, ny, nz, ch = own.shape
    if masks:
        kept, sent, grads, near_one, far_one, padded, moved, stacked, total, pairs = rest[4:]
        mine, theirs = both_columns(rest[:4])
        weights = placed_weights(spot, masks, mine, theirs, pairs)
    else:
        full, total, grads, near_one, far_one, padded, moved, stacked = rest
        weights = plain_weights(full)
    fill_padded(spot, padded, own, near, far)

    def finish(x, y, value):
        value = (value * slope[x, y]).astype(bf16)
        grads[x, y] = value
        value = value.astype(f32)
        at = (x * ny + y) * nz
        for k, c in enumerate(shifts):
            moved[at : at + nz, k * ch : (k + 1) * ch] = shift_rows(value, c).astype(bf16)

    data_layers(padded, weights, finish, range(nx))
    send_edges(spot, grads, near_one, far_one)
    stack_turned(stacked, turned_own, turned_sides)
    part = jnp.dot(stacked[...], moved[...], preferred_element_type=f32) * scale
    for i in range(len(planes)):
        for k in range(len(shifts)):
            at = (i * len(shifts) + k) * ch
            total[at : at + ch] = part[i * ch : (i + 1) * ch, k * ch : (k + 1) * ch]
    if masks:
        split_halves(total, spot[2], kept, sent)


def input_grads(spot, own, near, far, *rest, masks):
    if masks:
        lists, (out, padded, pairs) = rest[:4], rest[4:]
        mine, theirs = both_columns(lists)
        weights = placed_weights(spot, masks, mine, theirs, pairs)
    else:
        full, out, padded = rest
        weights = plain_weights(full)
    fill_padded(spot, padded, own, near, far)

    def finish(x, y, value):
        out[x, y] = value.astype(bf16)

    data_layers(padded, weights, finish, range(out.shape[0]))


def first_column(part, far_part, extra, pair, handed):
    pair[0] = part[...]
    pair[1] = far_part[...]
    handed[...] = extra[...]


def second_column(pair, near_pair, part, far_part, column, pair_next):
    column[0:2] = pair[...]
    column[2:4] = near_pair[...]
    pair_next[0] = part[...]
    pair_next[1] = far_part[...]


def halve(spot, kept, got, kept_next, sent_next, *, bit):
    side = spot[bit]
    for k in range(kept_next.shape[0]):
        mine, other = 2 * k + side, 2 * k + 1 - side
        kept_next[k] = kept[mine] + got[mine].astype(f32)
        sent_next[k] = (kept[other] + got[other].astype(f32)).astype(bf16)


def halve_and_stack(spot, kept, got, pair, other, across, kept_next, sent_next, column, handed, *, bit):
    handed[...] = across[...]
    halve(spot, kept, got, kept_next, sent_next, bit=bit)
    count = pair.shape[0]
    column[0:count] = pair[...]
    column[count:] = other[...]


def last_sum(kept, got, out):
    out[...] = kept[0] + got[0].astype(f32)


def call(body, n_smem, args, outs, scratch=(), after=(), us=0.2):
    first = len(args)
    many = len(after)

    def run(*refs):
        body(*refs[:first], *refs[first + many :])

    return pl.pallas_call(
        run if many else body,
        in_specs=[smem] * n_smem + [vmem] * (len(args) - n_smem) + [anywhere] * many,
        out_specs=[vmem] * len(outs),
        out_shape=[jax.ShapeDtypeStruct(s, d) for s, d in outs],
        scratch_shapes=[pltpu.VMEM(s, d) for s, d in scratch],
        cost_estimate=pl.CostEstimate(flops=int(us * 1e9), bytes_accessed=int(us * 3e6), transcendentals=0),
        compiler_params=pltpu.CompilerParams(vmem_limit_bytes=vmem_bytes),
    )(*args, *after)


def on_device(grad_out, inputs, pre_first, pre_second, filter_first, filter_second):
    shape = grad_out.shape
    nx, ny, nz, ch = shape
    n = lax.axis_size("gx")
    me = lax.axis_index("gx")
    rows = filter_first.shape[0]
    taps = n * rows // ch
    scale = 1.0 / math.sqrt(nx * n * ny * nz)
    spot = jnp.stack([me, jnp.full((), n, me.dtype), me % 2, me // 2 % 2, me // 4 % 2, me // 8 % 2]).astype(jnp.int32)
    fast = rows % 8 == 0 and n == 1 << 4
    masks = (0, 8, 4, 12, 2, 10, 6, 14) if fast else ()
    layer = (1,) + shape[1:]
    layers = (2,) + shape[1:]
    block = (rows, ch)
    wide = ((nx + 2, ny + 2, nz, ch), bf16)
    cells = nx * ny * nz
    total = ((taps * ch, ch), f32)

    def swap(array, mask):
        return lax.ppermute(array, "gx", [(i, i ^ mask) for i in range(n)])

    def swap_far(array):
        ahead = [(i, i + 1) for i in range(1, n - 1, 2)]
        return lax.ppermute(array, "gx", ahead + [(b, a) for a, b in ahead])

    def blocks(count, dtype=bf16):
        return ((count,) + block, dtype)

    turned, turned_own, slope = call(
        prepare,
        0,
        (pre_first, inputs),
        [((3 * ch, cells), bf16), ((nx, ny, ch, nz), bf16), (shape, f32)],
    )
    terms = [blocks(n // 2, f32), blocks(n // 2)] if fast else [total]
    work = [total, ((n // 2, 2 * rows, ch), bf16)] if fast else []

    after = (turned,)
    if fast:
        pair, handed = call(
            first_column,
            0,
            (filter_second, swap(filter_second, 8), filter_first),
            [blocks(2), (block, bf16)],
            after=after,
        )
        after = (pair,)
    grad_two, near, far = call(
        first_grads,
        1,
        (spot, grad_out, pre_second, inputs),
        [(shape, bf16)] + [(layers, bf16)] * 2,
        after=after,
    )
    far = swap_far(far)
    near = swap(near, 1)
    after = ()
    if fast:
        column, pair_first = call(
            second_column,
            0,
            (pair, swap(pair, 4), handed, swap(handed, 8)),
            [blocks(4), blocks(2)],
            after=(grad_two,),
        )
        after = (column,)
    *terms_two, turned_sides = call(
        functools.partial(second_filter, scale=scale, fast=fast),
        1,
        (spot, grad_two, near, far, turned),
        terms + [((2, ny, ch, nz), bf16)],
        [wide] + work[:1],
        after=after,
        us=2,
    )
    if fast:
        across = swap(column, 2)
        kept_two, sent_two, column_first, across = call(
            functools.partial(halve_and_stack, bit=3),
            1,
            (spot, terms_two[0], swap(terms_two[1], 1), pair_first, swap(pair_first, 4), across),
            [blocks(4, f32), blocks(4), blocks(4), blocks(4)],
        )
        full_second = (column, across, swap(column, 1), swap(across, 1))
    else:
        full_second = (lax.all_gather(filter_second, "gx", axis=0, tiled=True),)

    *terms_one, grad_one, near_one, far_one = call(
        functools.partial(first_filter, scale=scale, masks=masks),
        1,
        (spot, slope, grad_two, near, far, turned_own, turned_sides, *full_second),
        terms + [(shape, bf16), (layer, bf16), (layer, bf16)],
        [wide, ((cells, 3 * ch), bf16), ((len(planes) * ch, cells), bf16)] + work,
        us=8,
    )
    near_one, far_one = swap(near_one, 1), swap_far(far_one)

    def finish(full, after=()):
        return call(
            functools.partial(input_grads, masks=masks),
            1,
            (spot, grad_one, near_one, far_one, *full),
            [(shape, bf16)],
            [wide] + work[1:],
            after=after,
            us=3,
        )[0]

    if fast:

        def step(kept, sent, bit, mask, count, after):
            return call(
                functools.partial(halve, bit=bit),
                1,
                (spot, kept, swap(sent, mask)),
                [blocks(count, f32), blocks(count)],
                after=after,
            )

        kept_two, sent_two = step(kept_two, sent_two, 4, 2, 2, (grad_one,))
        kept_one, sent_one = step(*terms_one, 3, 1, 4, (kept_two,))
        kept_two, sent_two = step(kept_two, sent_two, 5, 4, 1, (kept_one,))
        kept_one, sent_one = step(kept_one, sent_one, 4, 2, 2, (kept_two,))
        kept_one, sent_one = step(kept_one, sent_one, 5, 4, 1, ())
        across_first = swap(column_first, 2)
        mine = (column_first, across_first)
        grad_in = finish((*mine, *(swap(m, 1) for m in mine)), (kept_one,))
        (owned_two,) = call(last_sum, 0, (kept_two, swap(sent_two, 8)), [(block, f32)])
        (owned_one,) = call(last_sum, 0, (kept_one, swap(sent_one, 8)), [(block, f32)], after=(grad_in,))
    else:
        grad_in = finish((lax.all_gather(filter_first, "gx", axis=0, tiled=True),))
        owned_two, owned_one = (
            lax.psum_scatter(t[0], "gx", scatter_dimension=0, tiled=True) for t in (terms_two, terms_one)
        )
    return (grad_in, owned_one, owned_two)


def solution(mesh):
    whole = P(("groups", "gx"), None, None, None)
    return jax.shard_map(
        on_device,
        mesh=mesh,
        in_specs=(whole, whole, whole, whole, P("gx", None), P("gx", None)),
        out_specs=(whole, P("gx", "groups"), P("gx", "groups")),
        check_vma=False,
    )
```

```python
import functools
import math

import jax
import jax.numpy as jnp
from jax import lax
from jax.experimental import pallas as pl
from jax.experimental.pallas import tpu as pltpu
from jax.sharding import PartitionSpec as P

inv_root_two = 0.7071067811865476
inv_root_twopi = 0.3989422804014327
shifts = (-1, 0, 1)
planes = tuple((a, b) for a in shifts for b in shifts)
bf16, f32 = jnp.bfloat16, jnp.float32
vmem = pl.BlockSpec(memory_space=pltpu.VMEM)
smem = pl.BlockSpec(memory_space=pltpu.SMEM)
anywhere = pl.BlockSpec(memory_space=pl.ANY)
vmem_bytes = 14 * 1024 * 1024


def cdf_of(value):
    return 0.5 * (1.0 + lax.erf(value * inv_root_two))


def slope_of(value):
    return cdf_of(value) + value * jnp.exp(-0.5 * value * value) * inv_root_twopi


def value_of(value):
    return value * cdf_of(value)


def shift_rows(block, c):
    rows = block.shape[0]
    if c == 0:
        return block
    place = lax.broadcasted_iota(jnp.int32, block.shape, 0)
    edge = 0 if c == 1 else rows - 1
    return jnp.where(place == edge, 0.0, pltpu.roll(block, c % rows, 0))


def zero_sides(ref):
    layers, wide = ref.shape[:2]
    blank = jnp.zeros(ref.shape[2:], ref.dtype)
    for x in range(layers):
        ref[x, 0] = blank
        ref[x, wide - 1] = blank


def first_grads(spot, grad_out, pre_second, inputs, own, near, far):
    nx = own.shape[0]
    for x in range(nx):
        for y in range(own.shape[1]):
            slope = slope_of(pre_second[x, y].astype(f32))
            own[x, y] = (grad_out[x, y].astype(f32) * slope).astype(bf16)
    send_edges(spot, own, near, far)
    at = near_edge(spot, nx - 1)
    near[1] = inputs[at]
    far[1] = inputs[nx - 1 - at]


def near_edge(spot, last):
    return last * (1 - spot[2])


def send_edges(spot, own, near, far):
    last = own.shape[0] - 1
    at = near_edge(spot, last)
    near[0] = own[at]
    far[0] = own[last - at]


def filter_terms(turned, padded, emit, scale):
    nx, ny = padded.shape[0] - 2, padded.shape[1] - 2
    nz, ch = padded.shape[2:]
    rows = nx * ny * nz

    def piece(a, b):
        return padded[1 - a : 1 - a + nx, 1 - b : 1 - b + ny].reshape(rows, ch)

    for i in range(0, len(planes), 2):
        pair = planes[i : i + 2]
        right = jnp.concatenate([piece(a, b) for a, b in pair], axis=1)
        part = jnp.dot(turned[...], right, preferred_element_type=f32) * scale
        for j in range(len(pair)):
            emit(i + j, part[:, j * ch : (j + 1) * ch])


def prepare(pre_first, inputs, turned, turned_own, slope):
    nx, ny, nz, ch = pre_first.shape
    for x in range(nx):
        for y in range(ny):
            value = pre_first[x, y].astype(f32)
            slope[x, y] = slope_of(value)
            block = value_of(value).astype(bf16).astype(f32)
            at = (x * ny + y) * nz
            for k, c in enumerate(shifts):
                turned[k * ch : (k + 1) * ch, at : at + nz] = shift_rows(block, -c).T.astype(bf16)
            turned_own[x, y] = inputs[x, y].astype(f32).T.astype(bf16)


def stack_turned(stacked, turned_own, turned_sides):
    nx, ny, ch, nz = turned_own.shape
    blank = jnp.zeros((ch, nz), bf16)
    for i, (a, b) in enumerate(planes):
        for x in range(nx):
            for y in range(ny):
                if 0 <= y + b < ny:
                    inside = 0 <= x + a < nx
                    block = turned_own[x + a, y + b] if inside else turned_sides[int(x + a == nx), y + b]
                else:
                    block = blank
                at = (x * ny + y) * nz
                stacked[i * ch : (i + 1) * ch, at : at + nz] = block


def data_layers(padded, weights, finish, out_x):
    ny = padded.shape[1] - 2
    nz, ch = padded.shape[2:]
    rows = ny * nz
    for x in out_x:
        total = None
        for i in range(0, len(planes), 2):
            pair = planes[i : i + 2]
            left = jnp.concatenate(
                [padded[1 + x - a, 1 - b : 1 - b + ny].reshape(rows, ch) for a, b in pair], axis=1
            )
            right = jnp.concatenate([weights(i + j) for j in range(len(pair))], axis=1)
            part = lax.dot_general(left, right, (((1,), (1,)), ((), ())), preferred_element_type=f32)
            total = part if total is None else total + part
        for y in range(ny):
            block = total[y * nz : (y + 1) * nz]
            value = sum(shift_rows(block[:, k * ch : (k + 1) * ch], c) for k, c in enumerate(shifts))
            finish(x, y, value)


def fill_padded(spot, padded, own, near, far):
    nx, ny = own.shape[:2]
    zero_sides(padded)
    padded[1 : 1 + nx, 1 : 1 + ny] = own[...]
    at = near_edge(spot, nx + 1)
    padded[at, 1 : 1 + ny] = near[0]
    padded[nx + 1 - at, 1 : 1 + ny] = far[0]


def widen(spot, own, near, far, padded):
    fill_padded(spot, padded, own, near, far)


def split_halves(total, side, kept, sent):
    half, rows = kept.shape[:2]
    for k in range(half):
        kept[k] = total[pl.ds(pl.multiple_of((2 * k + side) * rows, 8), rows)]
        sent[k] = total[pl.ds(pl.multiple_of((2 * k + 1 - side) * rows, 8), rows)].astype(bf16)


def plain_weights(full):
    ch = full.shape[1]
    return lambda plane: full[plane * 3 * ch : (plane + 1) * 3 * ch]


def placed_weights(spot, masks, mine, theirs, pairs):
    even = spot[2] == 0
    for mask, first, second in zip(masks, mine, theirs):
        one, two = first[...].astype(f32), second[...].astype(f32)
        both = jnp.concatenate([jnp.where(even, one, two), jnp.where(even, two, one)], axis=0)
        pairs[lax.bitwise_xor(spot[0] // 2, mask // 2)] = both.astype(bf16)
    wide, ch = pairs.shape[1:]

    def weights(plane):
        at, end = plane * 3 * ch, (plane + 1) * 3 * ch
        pieces = []
        while at < end:
            stop = min(end, (at // wide + 1) * wide)
            pieces.append(pairs[at // wide, at % wide : at % wide + stop - at])
            at = stop
        return jnp.concatenate(pieces, axis=0) if len(pieces) > 1 else pieces[0]

    return weights


def second_filter(spot, padded, near, far, turned, *rest, scale, fast):
    total, outs = (rest[-1], rest[:2]) if fast else (rest[0], ())
    turned_sides = rest[2] if fast else rest[1]
    ny = near.shape[1]

    def emit(plane, part):
        ch = part.shape[1]
        total[plane * 3 * ch : (plane + 1) * 3 * ch] = part

    filter_terms(turned, padded, emit, scale)
    if fast:
        split_halves(total, spot[2], *outs)
    high = near_edge(spot, 1)
    for y in range(ny):
        turned_sides[high, y] = near[1, y].astype(f32).T.astype(bf16)
        turned_sides[1 - high, y] = far[1, y].astype(f32).T.astype(bf16)


def both_columns(lists):
    split = [[ref.at[k] for k in range(ref.shape[0])] for ref in lists]
    return split[0] + split[1], split[2] + split[3]


def first_filter(spot, slope, padded, turned_own, turned_sides, *rest, scale, masks):
    nx, ny, nz, ch = slope.shape
    if masks:
        kept, sent, grads, near_one, far_one, moved, stacked, total, pairs = rest[4:]
        mine, theirs = both_columns(rest[:4])
        weights = placed_weights(spot, masks, mine, theirs, pairs)
    else:
        full, total, grads, near_one, far_one, moved, stacked = rest
        weights = plain_weights(full)

    def finish(x, y, value):
        value = (value * slope[x, y]).astype(bf16)
        grads[x, y] = value
        value = value.astype(f32)
        at = (x * ny + y) * nz
        for k, c in enumerate(shifts):
            moved[at : at + nz, k * ch : (k + 1) * ch] = shift_rows(value, c).astype(bf16)

    data_layers(padded, weights, finish, range(nx))
    send_edges(spot, grads, near_one, far_one)
    stack_turned(stacked, turned_own, turned_sides)
    part = jnp.dot(stacked[...], moved[...], preferred_element_type=f32) * scale
    for i in range(len(planes)):
        for k in range(len(shifts)):
            at = (i * len(shifts) + k) * ch
            total[at : at + ch] = part[i * ch : (i + 1) * ch, k * ch : (k + 1) * ch]
    if masks:
        split_halves(total, spot[2], kept, sent)


def input_grads(spot, own, near, far, *rest, masks):
    if masks:
        lists, (out, padded, pairs) = rest[:4], rest[4:]
        mine, theirs = both_columns(lists)
        weights = placed_weights(spot, masks, mine, theirs, pairs)
    else:
        full, out, padded = rest
        weights = plain_weights(full)
    fill_padded(spot, padded, own, near, far)

    def finish(x, y, value):
        out[x, y] = value.astype(bf16)

    data_layers(padded, weights, finish, range(out.shape[0]))


def stack(*refs, counts):
    ins, outs = refs[: sum(counts)], refs[sum(counts) :]
    for count, out in zip(counts, outs):
        at = 0
        for part in ins[:count]:
            if len(part.shape) < len(out.shape):
                out[at] = part[...]
                at += 1
            else:
                out[at : at + part.shape[0]] = part[...]
                at += part.shape[0]
        ins = ins[count:]


def halve(spot, kept, got, kept_next, sent_next, *, bit):
    side = spot[bit]
    for k in range(kept_next.shape[0]):
        mine, other = 2 * k + side, 2 * k + 1 - side
        kept_next[k] = kept[mine] + got[mine].astype(f32)
        sent_next[k] = (kept[other] + got[other].astype(f32)).astype(bf16)


def halve_both(spot, kept_a, got_a, kept_b, got_b, next_a, send_a, next_b, send_b, *, bit_a, bit_b):
    halve(spot, kept_b, got_b, next_b, send_b, bit=bit_b)
    halve(spot, kept_a, got_a, next_a, send_a, bit=bit_a)


def last_sum(kept, got, out):
    out[...] = kept[0] + got[0].astype(f32)


def last_sums(kept_a, got_a, kept_b, got_b, out_a, out_b):
    last_sum(kept_a, got_a, out_a)
    last_sum(kept_b, got_b, out_b)


def call(body, n_smem, args, outs, scratch=(), after=(), us=0.2):
    first = len(args)
    many = len(after)

    def run(*refs):
        body(*refs[:first], *refs[first + many :])

    return pl.pallas_call(
        run if many else body,
        in_specs=[smem] * n_smem + [vmem] * (len(args) - n_smem) + [anywhere] * many,
        out_specs=[vmem] * len(outs),
        out_shape=[jax.ShapeDtypeStruct(s, d) for s, d in outs],
        scratch_shapes=[pltpu.VMEM(s, d) for s, d in scratch],
        cost_estimate=pl.CostEstimate(flops=int(us * 1e9), bytes_accessed=int(us * 3e6), transcendentals=0),
        compiler_params=pltpu.CompilerParams(vmem_limit_bytes=vmem_bytes),
    )(*args, *after)


def on_device(grad_out, inputs, pre_first, pre_second, filter_first, filter_second):
    shape = grad_out.shape
    nx, ny, nz, ch = shape
    n = lax.axis_size("gx")
    me = lax.axis_index("gx")
    rows = filter_first.shape[0]
    taps = n * rows // ch
    scale = 1.0 / math.sqrt(nx * n * ny * nz)
    spot = jnp.stack([me, jnp.full((), n, me.dtype), me % 2, me // 2 % 2, me // 4 % 2, me // 8 % 2]).astype(jnp.int32)
    fast = rows % 8 == 0 and n == 1 << 4
    masks_two = (0, 8, 4, 12, 2, 10, 6, 14) if fast else ()
    masks_one = (0, 2, 8, 10, 4, 6, 12, 14) if fast else ()
    layer = (1,) + shape[1:]
    layers = (2,) + shape[1:]
    block = (rows, ch)
    wide = ((nx + 2, ny + 2, nz, ch), bf16)
    cells = nx * ny * nz
    total = ((taps * ch, ch), f32)

    def swap(array, mask):
        return lax.ppermute(array, "gx", [(i, i ^ mask) for i in range(n)])

    def swap_far(array):
        ahead = [(i, i + 1) for i in range(1, n - 1, 2)]
        return lax.ppermute(array, "gx", ahead + [(b, a) for a, b in ahead])

    def blocks(count, dtype=bf16):
        return ((count,) + block, dtype)

    def stacked(groups, sizes, after, us=0.2):
        parts = [part for group in groups for part in group]
        body = functools.partial(stack, counts=[len(group) for group in groups])
        return call(body, 0, parts, [blocks(size) for size in sizes], after=after, us=us)

    terms = [blocks(n // 2, f32), blocks(n // 2)] if fast else [total]
    work = [total, ((n // 2, 2 * rows, ch), bf16)] if fast else []

    grad_two, near, far = call(
        first_grads, 1, (spot, grad_out, pre_second, inputs), [(shape, bf16)] + [(layers, bf16)] * 2, us=20
    )
    far = swap_far(far)
    near = swap(near, 1)
    after = (grad_two,)
    if fast:
        pair, pair_first = stacked(
            [(filter_second, swap(filter_second, 8)), (filter_first, swap(filter_first, 2))], (2, 2), after
        )
        after = (pair,)
    turned, turned_own, slope = call(
        prepare,
        0,
        (pre_first, inputs),
        [((3 * ch, cells), bf16), ((nx, ny, ch, nz), bf16), (shape, f32)],
        after=after,
        us=4,
    )
    (grads_wide,) = call(widen, 1, (spot, grad_two, near, far), [wide], after=(turned,), us=20)
    after = ()
    if fast:
        column, pair_first = stacked([(pair, swap(pair, 4)), (pair_first,)], (4, 2), (grads_wide,), 20)
        after = (column,)
    *terms_two, turned_sides = call(
        functools.partial(second_filter, scale=scale, fast=fast),
        1,
        (spot, grads_wide, near, far, turned),
        terms + [((2, ny, ch, nz), bf16)],
        work[:1],
        after=after,
        us=2,
    )
    if fast:
        across = swap(column, 2)
        across, column_first = stacked([(swap(column, 2),), (pair_first, swap(pair_first, 8))], (4, 4), (turned_sides,), 20)
        kept_two, sent_two = call(
            functools.partial(halve, bit=3),
            1,
            (spot, terms_two[0], swap(terms_two[1], 1)),
            [blocks(4, f32), blocks(4)],
            after=(across,),
        )
        full_second = (column, across, swap(column, 1), swap(across, 1))
        after = (kept_two,)
    else:
        after = ()
        full_second = (lax.all_gather(filter_second, "gx", axis=0, tiled=True),)

    *terms_one, grad_one, near_one, far_one = call(
        functools.partial(first_filter, scale=scale, masks=masks_two),
        1,
        (spot, slope, grads_wide, turned_own, turned_sides, *full_second),
        terms + [(shape, bf16), (layer, bf16), (layer, bf16)],
        [((cells, 3 * ch), bf16), ((len(planes) * ch, cells), bf16)] + work,
        after=after,
        us=8,
    )
    near_one, far_one = swap(near_one, 1), swap_far(far_one)

    def finish(full, after=()):
        return call(
            functools.partial(input_grads, masks=masks_one),
            1,
            (spot, grad_one, near_one, far_one, *full),
            [(shape, bf16)],
            [wide] + work[1:],
            after=after,
            us=5,
        )[0]

    if fast:


        def step(kept, sent, bit, mask, count, after, us=0.2):
            return call(
                functools.partial(halve, bit=bit),
                1,
                (spot, kept, swap(sent, mask)),
                [blocks(count, f32), blocks(count)],
                after=after,
                us=us,
            )

        kept_two, sent_two = step(kept_two, sent_two, 4, 2, 2, (grad_one,), 20)
        kept_one, sent_one = step(*terms_one, 3, 1, 4, (kept_two,))
        mine = (column_first, swap(column_first, 4))
        kept_two, sent_two, kept_one, sent_one = call(
            functools.partial(halve_both, bit_a=5, bit_b=4),
            1,
            (spot, kept_two, swap(sent_two, 4), kept_one, swap(sent_one, 2)),
            [blocks(1, f32), blocks(1), blocks(2, f32), blocks(2)],
            us=20,
        )
        kept_one, sent_one = step(kept_one, sent_one, 5, 4, 1, ())
        grad_in = finish((*mine, *(swap(m, 1) for m in mine)), (kept_one,))
        owned_two, owned_one = call(
            last_sums,
            0,
            (kept_two, swap(sent_two, 8), kept_one, swap(sent_one, 8)),
            [(block, f32)] * 2,
            after=(grad_in,),
        )
    else:
        grad_in = finish((lax.all_gather(filter_first, "gx", axis=0, tiled=True),))
        owned_two, owned_one = (
            lax.psum_scatter(t[0], "gx", scatter_dimension=0, tiled=True) for t in (terms_two, terms_one)
        )
    return (grad_in, owned_one, owned_two)


def solution(mesh):
    whole = P(("groups", "gx"), None, None, None)
    return jax.shard_map(
        on_device,
        mesh=mesh,
        in_specs=(whole, whole, whole, whole, P("gx", None), P("gx", None)),
        out_specs=(whole, P("gx", "groups"), P("gx", "groups")),
        check_vma=False,
    )
```

```python
import functools
import math

import jax
import jax.numpy as jnp
from jax import lax
from jax.experimental import pallas as pl
from jax.experimental.pallas import tpu as pltpu
from jax.sharding import PartitionSpec as P

inv_root_two = 0.7071067811865476
inv_root_twopi = 0.3989422804014327
shifts = (-1, 0, 1)
planes = tuple((a, b) for a in shifts for b in shifts)
bf16, f32 = jnp.bfloat16, jnp.float32
vmem = pl.BlockSpec(memory_space=pltpu.VMEM)
anywhere = pl.BlockSpec(memory_space=pl.ANY)
vmem_bytes = 14 * 1024 * 1024


def cdf_of(value):
    return 0.5 * (1.0 + lax.erf(value * inv_root_two))


def slope_of(value):
    return cdf_of(value) + value * jnp.exp(-0.5 * value * value) * inv_root_twopi


def value_of(value):
    return value * cdf_of(value)


def shift_rows(block, c):
    rows = block.shape[0]
    if c == 0:
        return block
    place = lax.broadcasted_iota(jnp.int32, block.shape, 0)
    edge = 0 if c == 1 else rows - 1
    return jnp.where(place == edge, 0.0, pltpu.roll(block, c % rows, 0))


def zero_sides(ref):
    layers, wide = ref.shape[:2]
    blank = jnp.zeros(ref.shape[2:], ref.dtype)
    for x in range(layers):
        ref[x, 0] = blank
        ref[x, wide - 1] = blank


def first_grads(spot, grad_out, pre_second, own, near, far):
    nx = own.shape[0]
    for x in range(nx):
        for y in range(own.shape[1]):
            slope = slope_of(pre_second[x, y].astype(f32))
            own[x, y] = (grad_out[x, y].astype(f32) * slope).astype(bf16)
    send_edges(spot, own, near, far)


def near_edge(spot, last):
    return last * (1 - spot[1])


def send_edges(spot, own, near, far):
    last = own.shape[0] - 1
    at = near_edge(spot, last)
    near[0] = own[at]
    far[0] = own[last - at]


def filter_terms(turned, padded, emit, scale):
    nx, ny = padded.shape[0] - 2, padded.shape[1] - 2
    nz, ch = padded.shape[2:]
    rows = nx * ny * nz

    def piece(a, b):
        return padded[1 - a : 1 - a + nx, 1 - b : 1 - b + ny].reshape(rows, ch)

    for i in range(0, len(planes), 2):
        pair = planes[i : i + 2]
        right = jnp.concatenate([piece(a, b) for a, b in pair], axis=1)
        part = jnp.dot(turned[...], right, preferred_element_type=f32) * scale
        for j in range(len(pair)):
            emit(i + j, part[:, j * ch : (j + 1) * ch])


def prepare(spot, pre_first, inputs, turned, turned_own, slope):
    nx, ny, nz, ch = pre_first.shape
    for x in range(nx):
        for y in range(ny):
            value = pre_first[x, y].astype(f32)
            slope[x, y] = slope_of(value)
            block = value_of(value).astype(bf16).astype(f32)
            at = (x * ny + y) * nz
            for k, c in enumerate(shifts):
                turned[k * ch : (k + 1) * ch, at : at + nz] = shift_rows(block, -c).T.astype(bf16)
            turned_own[x, y] = inputs[x, y].astype(f32).T.astype(bf16)


def stack_turned(stacked, turned_own, turned_sides):
    nx, ny, ch, nz = turned_own.shape
    blank = jnp.zeros((ch, nz), bf16)
    for i, (a, b) in enumerate(planes):
        for x in range(nx):
            for y in range(ny):
                if 0 <= y + b < ny:
                    inside = 0 <= x + a < nx
                    block = turned_own[x + a, y + b] if inside else turned_sides[int(x + a == nx), y + b]
                else:
                    block = blank
                at = (x * ny + y) * nz
                stacked[i * ch : (i + 1) * ch, at : at + nz] = block


def data_layers(padded, weights, finish, out_x):
    ny = padded.shape[1] - 2
    nz, ch = padded.shape[2:]
    rows = ny * nz
    for x in out_x:
        total = None
        for i in range(0, len(planes), 2):
            pair = planes[i : i + 2]
            left = jnp.concatenate(
                [padded[1 + x - a, 1 - b : 1 - b + ny].reshape(rows, ch) for a, b in pair], axis=1
            )
            right = jnp.concatenate([weights(i + j) for j in range(len(pair))], axis=1)
            part = lax.dot_general(left, right, (((1,), (1,)), ((), ())), preferred_element_type=f32)
            total = part if total is None else total + part
        for y in range(ny):
            block = total[y * nz : (y + 1) * nz]
            value = sum(shift_rows(block[:, k * ch : (k + 1) * ch], c) for k, c in enumerate(shifts))
            finish(x, y, value)


def fill_padded(spot, padded, own, near, far):
    nx, ny = own.shape[:2]
    zero_sides(padded)
    padded[1 : 1 + nx, 1 : 1 + ny] = own[...]
    at = near_edge(spot, nx + 1)
    padded[at, 1 : 1 + ny] = near[0]
    padded[nx + 1 - at, 1 : 1 + ny] = far[0]


def widen(spot, own, near, far, padded):
    fill_padded(spot, padded, own, near, far)


def split_halves(total, side, kept, sent):
    half, rows = kept.shape[:2]
    for k in range(half):
        kept[k] = total[pl.ds(pl.multiple_of((2 * k + side) * rows, 8), rows)]
        sent[k] = total[pl.ds(pl.multiple_of((2 * k + 1 - side) * rows, 8), rows)].astype(bf16)


def plain_weights(full):
    ch = full.shape[1]
    return lambda plane: full[plane * 3 * ch : (plane + 1) * 3 * ch]


def placed_weights(spot, masks, mine, theirs, pairs):
    even = spot[1] == 0
    for mask, first, second in zip(masks, mine, theirs):
        one, two = first[...].astype(f32), second[...].astype(f32)
        both = jnp.concatenate([jnp.where(even, one, two), jnp.where(even, two, one)], axis=0)
        pairs[lax.bitwise_xor(spot[0] >> 1, mask // 2)] = both.astype(bf16)
    wide, ch = pairs.shape[1:]

    def weights(plane):
        at, end = plane * 3 * ch, (plane + 1) * 3 * ch
        pieces = []
        while at < end:
            stop = min(end, (at // wide + 1) * wide)
            pieces.append(pairs[at // wide, at % wide : at % wide + stop - at])
            at = stop
        return jnp.concatenate(pieces, axis=0) if len(pieces) > 1 else pieces[0]

    return weights


def second_filter(spot, padded, turned, *rest, scale, fast):
    total, outs = (rest[-1], rest[:2]) if fast else (rest[0], ())

    def emit(plane, part):
        ch = part.shape[1]
        total[plane * 3 * ch : (plane + 1) * 3 * ch] = part

    filter_terms(turned, padded, emit, scale)
    if fast:
        split_halves(total, spot[1], *outs)

def turn_sides(spot, near, far, turned_sides):
    high = near_edge(spot, 1)
    for y in range(near.shape[1]):
        turned_sides[high, y] = near[0, y].astype(f32).T.astype(bf16)
        turned_sides[1 - high, y] = far[0, y].astype(f32).T.astype(bf16)


def stack_and_edges(spot, pair, other, inputs, column, near, far):
    count = pair.shape[0]
    column[0:count] = pair[...]
    column[count:] = other[...]
    send_edges(spot, inputs, near, far)


def both_columns(lists):
    split = [[ref.at[k] for k in range(ref.shape[0])] for ref in lists]
    return split[0] + split[1], split[2] + split[3]


def first_filter(spot, slope, padded, turned_own, turned_sides, *rest, scale, masks):
    nx, ny, nz, ch = slope.shape
    if masks:
        kept, sent, grads, near_one, far_one, moved, stacked, total, pairs = rest[4:]
        mine, theirs = both_columns(rest[:4])
        weights = placed_weights(spot, masks, mine, theirs, pairs)
    else:
        full, total, grads, near_one, far_one, moved, stacked = rest
        weights = plain_weights(full)

    def finish(x, y, value):
        value = (value * slope[x, y]).astype(bf16)
        grads[x, y] = value
        value = value.astype(f32)
        at = (x * ny + y) * nz
        for k, c in enumerate(shifts):
            moved[at : at + nz, k * ch : (k + 1) * ch] = shift_rows(value, c).astype(bf16)

    data_layers(padded, weights, finish, range(nx))
    send_edges(spot, grads, near_one, far_one)
    stack_turned(stacked, turned_own, turned_sides)
    part = jnp.dot(stacked[...], moved[...], preferred_element_type=f32) * scale
    for i in range(len(planes)):
        for k in range(len(shifts)):
            at = (i * len(shifts) + k) * ch
            total[at : at + ch] = part[i * ch : (i + 1) * ch, k * ch : (k + 1) * ch]
    if masks:
        split_halves(total, spot[1], kept, sent)


def input_grads(spot, own, near, far, *rest, masks):
    if masks:
        lists, rest = rest[:4], rest[4:]
        (padded, pairs), rest = rest[-2:], rest[:-2]
        kept, kept_two, got_two, out, kept_on, sum_two = rest
        kept_on[...] = kept[...]
        last_sum(kept_two, got_two, sum_two)
        mine, theirs = both_columns(lists)
        weights = placed_weights(spot, masks, mine, theirs, pairs)
    else:
        full, out, padded = rest
        weights = plain_weights(full)
    fill_padded(spot, padded, own, near, far)

    def finish(x, y, value):
        out[x, y] = value.astype(bf16)

    data_layers(padded, weights, finish, range(out.shape[0]))


def stack(*refs, counts):
    ins, outs = refs[: sum(counts)], refs[sum(counts) :]
    for count, out in zip(counts, outs):
        at = 0
        for part in ins[:count]:
            if len(part.shape) < len(out.shape):
                out[at] = part[...]
                at += 1
            else:
                out[at : at + part.shape[0]] = part[...]
                at += part.shape[0]
        ins = ins[count:]


def halve(spot, kept, got, kept_next, sent_next, *, bit):
    side = spot[bit - 1]
    for k in range(kept_next.shape[0]):
        mine, other = 2 * k + side, 2 * k + 1 - side
        kept_next[k] = kept[mine] + got[mine].astype(f32)
        sent_next[k] = (kept[other] + got[other].astype(f32)).astype(bf16)


def halve_and_pass(spot, kept, got, near, far, kept_next, sent_next, near_on, far_on, *, bit):
    halve(spot, kept, got, kept_next, sent_next, bit=bit)
    near_on[...] = near[...]
    far_on[...] = far[...]


def last_sum(kept, got, out):
    out[...] = kept[0] + got[0].astype(f32)


def call(body, n_smem, args, outs, scratch=(), after=(), us=0.2):
    args = args[n_smem:]
    first, many = len(args), len(after)

    def run(*refs):
        refs = refs[:first] + refs[first + many :]
        if n_smem:
            me = lax.axis_index("gx")
            body([me] + [(me >> k) & 1 for k in range(4)], *refs)
        else:
            body(*refs)

    return pl.pallas_call(
        run,
        in_specs=[vmem] * first + [anywhere] * many,
        out_specs=[vmem] * len(outs),
        out_shape=[jax.ShapeDtypeStruct(s, d) for s, d in outs],
        scratch_shapes=[pltpu.VMEM(s, d) for s, d in scratch],
        cost_estimate=pl.CostEstimate(flops=int(us * 1e9), bytes_accessed=int(us * 3e6), transcendentals=0),
        compiler_params=pltpu.CompilerParams(vmem_limit_bytes=vmem_bytes),
    )(*args, *after)


def on_device(grad_out, inputs, pre_first, pre_second, filter_first, filter_second):
    shape = grad_out.shape
    nx, ny, nz, ch = shape
    n = lax.axis_size("gx")
    me = lax.axis_index("gx")
    rows = filter_first.shape[0]
    taps = n * rows // ch
    scale = 1.0 / math.sqrt(nx * n * ny * nz)
    spot = None
    fast = rows % 8 == 0 and n == 1 << 4
    masks_two = (0, 8, 4, 12, 2, 10, 6, 14) if fast else ()
    masks_one = (0, 2, 8, 10, 4, 6, 12, 14) if fast else ()
    layer = (1,) + shape[1:]
    block = (rows, ch)
    wide = ((nx + 2, ny + 2, nz, ch), bf16)
    cells = nx * ny * nz
    total = ((taps * ch, ch), f32)

    def swap(array, mask):
        return lax.ppermute(array, "gx", [(i, i ^ mask) for i in range(n)])

    def swap_far(array):
        ahead = [(i, i + 1) for i in range(1, n - 1, 2)]
        return lax.ppermute(array, "gx", ahead + [(b, a) for a, b in ahead])

    def blocks(count, dtype=bf16):
        return ((count,) + block, dtype)

    def stacked(groups, sizes, after, us=0.2):
        parts = [part for group in groups for part in group]
        body = functools.partial(stack, counts=[len(group) for group in groups])
        return call(body, 0, parts, [blocks(size) for size in sizes], after=after, us=us)

    terms = [blocks(n // 2, f32), blocks(n // 2)] if fast else [total]
    work = [total, ((n // 2, 2 * rows, ch), bf16)] if fast else []

    grad_two, near, far = call(
        first_grads, 1, (spot, grad_out, pre_second), [(shape, bf16), (layer, bf16), (layer, bf16)], us=20
    )
    far = swap_far(far)
    near = swap(near, 1)
    after = (grad_two,)
    if fast:
        pair, pair_first = stacked(
            [(filter_second, swap(filter_second, 8)), (filter_first, swap(filter_first, 2))], (2, 2), after
        )
        after = (pair,)
    turned, turned_own, slope = call(
        prepare,
        1,
        (spot, pre_first, inputs),
        [((3 * ch, cells), bf16), ((nx, ny, ch, nz), bf16), (shape, f32)],
        after=after,
        us=4,
    )
    (grads_wide,) = call(widen, 1, (spot, grad_two, near, far), [wide], after=(turned,), us=20)
    sides = ((2, ny, ch, nz), bf16)
    if fast:
        column, near_in, far_in = call(
            stack_and_edges,
            1,
            (spot, pair, swap(pair, 4), inputs),
            [blocks(4), (layer, bf16), (layer, bf16)],
            after=(grads_wide,),
            us=20,
        )
        after = (column,)
    else:
        near_in, far_in = call(send_edges, 1, (spot, inputs), [(layer, bf16), (layer, bf16)])
        after = ()
    terms_two = call(
        functools.partial(second_filter, scale=scale, fast=fast),
        1,
        (spot, grads_wide, turned),
        terms,
        work[:1],
        after=after,
        us=2,
    )
    near_in, far_in = swap(near_in, 1), swap_far(far_in)
    if fast:
        across = swap(column, 2)
        after = (across,)
    else:
        full_second = (lax.all_gather(filter_second, "gx", axis=0, tiled=True),)
        after = ()
    (turned_sides,) = call(turn_sides, 1, (spot, near_in, far_in), [sides], after=after, us=20)
    if fast:
        kept_two, sent_two = call(
            functools.partial(halve, bit=3),
            1,
            (spot, terms_two[0], swap(terms_two[1], 1)),
            [blocks(4, f32), blocks(4)],
            after=(turned_sides,),
        )
        (column_first,) = stacked([(pair_first, swap(pair_first, 8))], (4,), (kept_two,))
        after = (column_first,)
        full_second = (column, across, swap(column, 1), swap(across, 1))

    *terms_one, grad_one, near_one, far_one = call(
        functools.partial(first_filter, scale=scale, masks=masks_two),
        1,
        (spot, slope, grads_wide, turned_own, turned_sides, *full_second),
        terms + [(shape, bf16), (layer, bf16), (layer, bf16)],
        [((cells, 3 * ch), bf16), ((len(planes) * ch, cells), bf16)] + work,
        after=after,
        us=8,
    )

    def finish(near, far, full, sums=()):
        sizes = [blocks(1, f32), (block, f32)] if sums else []
        return call(
            functools.partial(input_grads, masks=masks_one),
            1,
            (spot, grad_one, swap(near, 1), swap_far(far), *full, *sums),
            [(shape, bf16)] + sizes,
            [wide] + work[1:],
            us=5,
        )

    if fast:

        def step(kept, sent, bit, mask, count, after, us=0.2):
            return call(
                functools.partial(halve, bit=bit),
                1,
                (spot, kept, swap(sent, mask)),
                [blocks(count, f32), blocks(count)],
                after=after,
                us=us,
            )

        kept_two, sent_two = step(kept_two, sent_two, 4, 2, 2, (grad_one,), 20)
        kept_one, sent_one = step(*terms_one, 3, 1, 4, (kept_two,))
        mine = (column_first, swap(column_first, 4))
        full_first = (*mine, *(swap(m, 1) for m in mine))
        kept_two, sent_two = step(kept_two, sent_two, 5, 4, 1, (kept_one, *full_first), 20)
        got_two = swap(sent_two, 8)
        kept_one, sent_one, near_one, far_one = call(
            functools.partial(halve_and_pass, bit=4),
            1,
            (spot, kept_one, swap(sent_one, 2), near_one, far_one),
            [blocks(2, f32), blocks(2), (layer, bf16), (layer, bf16)],
            after=(kept_two,),
            us=20,
        )
        kept_one, sent_one = step(kept_one, sent_one, 5, 4, 1, (), 1.5)
        grad_in, kept_one, owned_two = finish(
            near_one, far_one, full_first, (kept_one, kept_two, got_two)
        )
        (owned_one,) = call(last_sum, 0, (kept_one, swap(sent_one, 8)), [(block, f32)])
    else:
        (grad_in,) = finish(near_one, far_one, (lax.all_gather(filter_first, "gx", axis=0, tiled=True),))
        owned_two, owned_one = (
            lax.psum_scatter(t[0], "gx", scatter_dimension=0, tiled=True) for t in (terms_two, terms_one)
        )
    return (grad_in, owned_one, owned_two)


def solution(mesh):
    whole = P(("groups", "gx"), None, None, None)
    return jax.shard_map(
        on_device,
        mesh=mesh,
        in_specs=(whole, whole, whole, whole, P("gx", None), P("gx", None)),
        out_specs=(whole, P("gx", "groups"), P("gx", "groups")),
        check_vma=False,
    )
```

```python
import functools
import math

import jax
import jax.numpy as jnp
from jax import lax
from jax.experimental import pallas as pl
from jax.experimental.pallas import tpu as pltpu
from jax.sharding import PartitionSpec as P

inv_root_two = 0.7071067811865476
inv_root_twopi = 0.3989422804014327
shifts = (-1, 0, 1)
planes = tuple((a, b) for a in shifts for b in shifts)
bf16, f32 = jnp.bfloat16, jnp.float32
vmem = pl.BlockSpec(memory_space=pltpu.VMEM)
anywhere = pl.BlockSpec(memory_space=pl.ANY)
vmem_bytes = 14 * 1024 * 1024


def cdf_of(value):
    return 0.5 * (1.0 + lax.erf(value * inv_root_two))


def slope_of(value):
    return cdf_of(value) + value * jnp.exp(-0.5 * value * value) * inv_root_twopi


def value_of(value):
    return value * cdf_of(value)


def shift_rows(block, c):
    rows = block.shape[0]
    if c == 0:
        return block
    place = lax.broadcasted_iota(jnp.int32, block.shape, 0)
    edge = 0 if c == 1 else rows - 1
    return jnp.where(place == edge, 0.0, pltpu.roll(block, c % rows, 0))


def zero_sides(ref):
    layers, wide = ref.shape[:2]
    blank = jnp.zeros(ref.shape[2:], ref.dtype)
    for x in range(layers):
        ref[x, 0] = blank
        ref[x, wide - 1] = blank


def near_edge(spot, last):
    return last * (1 - spot[1])


def send_edges(spot, own, near, far):
    last = own.shape[0] - 1
    at = near_edge(spot, last)
    near[0] = own[at]
    far[0] = own[last - at]


def filter_terms(turned, padded, emit, scale):
    nx, ny = padded.shape[0] - 2, padded.shape[1] - 2
    nz, ch = padded.shape[2:]
    rows = nx * ny * nz

    def piece(a, b):
        return padded[1 - a : 1 - a + nx, 1 - b : 1 - b + ny].reshape(rows, ch)

    for i in range(0, len(planes), 2):
        pair = planes[i : i + 2]
        right = jnp.concatenate([piece(a, b) for a, b in pair], axis=1)
        part = jnp.dot(turned[...], right, preferred_element_type=f32) * scale
        for j in range(len(pair)):
            emit(i + j, part[:, j * ch : (j + 1) * ch])


def prepare(spot, pre_first, inputs, turned, turned_own, slope):
    nx, ny, nz, ch = pre_first.shape
    for x in range(nx):
        for y in range(ny):
            value = pre_first[x, y].astype(f32)
            slope[x, y] = slope_of(value)
            block = value_of(value).astype(bf16).astype(f32)
            at = (x * ny + y) * nz
            for k, c in enumerate(shifts):
                turned[k * ch : (k + 1) * ch, at : at + nz] = shift_rows(block, -c).T.astype(bf16)
            turned_own[x, y] = inputs[x, y].astype(f32).T.astype(bf16)


def stack_turned(stacked, turned_own, turned_sides):
    nx, ny, ch, nz = turned_own.shape
    blank = jnp.zeros((ch, nz), bf16)
    for i, (a, b) in enumerate(planes):
        for x in range(nx):
            for y in range(ny):
                if 0 <= y + b < ny:
                    inside = 0 <= x + a < nx
                    block = turned_own[x + a, y + b] if inside else turned_sides[int(x + a == nx), y + b]
                else:
                    block = blank
                at = (x * ny + y) * nz
                stacked[i * ch : (i + 1) * ch, at : at + nz] = block


def data_layers(padded, weights, finish, out_x):
    ny = padded.shape[1] - 2
    nz, ch = padded.shape[2:]
    rows = ny * nz
    for x in out_x:
        total = None
        for i in range(0, len(planes), 2):
            pair = planes[i : i + 2]
            left = jnp.concatenate(
                [padded[1 + x - a, 1 - b : 1 - b + ny].reshape(rows, ch) for a, b in pair], axis=1
            )
            right = jnp.concatenate([weights(i + j) for j in range(len(pair))], axis=1)
            part = lax.dot_general(left, right, (((1,), (1,)), ((), ())), preferred_element_type=f32)
            total = part if total is None else total + part
        for y in range(ny):
            block = total[y * nz : (y + 1) * nz]
            value = sum(shift_rows(block[:, k * ch : (k + 1) * ch], c) for k, c in enumerate(shifts))
            finish(x, y, value)


def fill_padded(spot, padded, own, near, far):
    nx, ny = own.shape[:2]
    zero_sides(padded)
    padded[1 : 1 + nx, 1 : 1 + ny] = own[...]
    at = near_edge(spot, nx + 1)
    padded[at, 1 : 1 + ny] = near[0]
    padded[nx + 1 - at, 1 : 1 + ny] = far[0]


def widen(spot, own, near, far, padded):
    fill_padded(spot, padded, own, near, far)


def split_halves(total, side, kept, sent):
    half, rows = kept.shape[:2]
    for k in range(half):
        kept[k] = total[pl.ds(pl.multiple_of((2 * k + side) * rows, 8), rows)]
        sent[k] = total[pl.ds(pl.multiple_of((2 * k + 1 - side) * rows, 8), rows)].astype(bf16)


def plain_weights(full):
    ch = full.shape[1]
    return lambda plane: full[plane * 3 * ch : (plane + 1) * 3 * ch]


def placed_weights(spot, masks, mine, theirs, pairs):
    even = spot[1] == 0
    for mask, first, second in zip(masks, mine, theirs):
        one, two = first[...].astype(f32), second[...].astype(f32)
        both = jnp.concatenate([jnp.where(even, one, two), jnp.where(even, two, one)], axis=0)
        pairs[lax.bitwise_xor(spot[0] >> 1, mask // 2)] = both.astype(bf16)
    wide, ch = pairs.shape[1:]

    def weights(plane):
        at, end = plane * 3 * ch, (plane + 1) * 3 * ch
        pieces = []
        while at < end:
            stop = min(end, (at // wide + 1) * wide)
            pieces.append(pairs[at // wide, at % wide : at % wide + stop - at])
            at = stop
        return jnp.concatenate(pieces, axis=0) if len(pieces) > 1 else pieces[0]

    return weights


def second_filter(spot, padded, turned, *rest, scale, fast):
    total, outs = (rest[-1], rest[:2]) if fast else (rest[0], ())

    def emit(plane, part):
        ch = part.shape[1]
        total[plane * 3 * ch : (plane + 1) * 3 * ch] = part

    filter_terms(turned, padded, emit, scale)
    if fast:
        split_halves(total, spot[1], *outs)

def turn_sides(spot, near, far, turned_sides):
    high = near_edge(spot, 1)
    for y in range(near.shape[1]):
        turned_sides[high, y] = near[0, y].astype(f32).T.astype(bf16)
        turned_sides[1 - high, y] = far[0, y].astype(f32).T.astype(bf16)


def stack_and_edges(spot, pair, other, inputs, column, near, far):
    count = pair.shape[0]
    column[0:count] = pair[...]
    column[count:] = other[...]
    send_edges(spot, inputs, near, far)


def both_columns(lists):
    split = [[ref.at[k] for k in range(ref.shape[0])] for ref in lists]
    return split[0] + split[1], split[2] + split[3]


def first_filter(spot, slope, padded, turned_own, turned_sides, *rest, scale, masks):
    nx, ny, nz, ch = slope.shape
    if masks:
        kept, sent, grads, near_one, far_one, moved, stacked, total, pairs = rest[4:]
        mine, theirs = both_columns(rest[:4])
        weights = placed_weights(spot, masks, mine, theirs, pairs)
    else:
        full, total, grads, near_one, far_one, moved, stacked = rest
        weights = plain_weights(full)

    def finish(x, y, value):
        value = (value * slope[x, y]).astype(bf16)
        grads[x, y] = value
        value = value.astype(f32)
        at = (x * ny + y) * nz
        for k, c in enumerate(shifts):
            moved[at : at + nz, k * ch : (k + 1) * ch] = shift_rows(value, c).astype(bf16)

    data_layers(padded, weights, finish, range(nx))
    send_edges(spot, grads, near_one, far_one)
    stack_turned(stacked, turned_own, turned_sides)
    part = jnp.dot(stacked[...], moved[...], preferred_element_type=f32) * scale
    for i in range(len(planes)):
        for k in range(len(shifts)):
            at = (i * len(shifts) + k) * ch
            total[at : at + ch] = part[i * ch : (i + 1) * ch, k * ch : (k + 1) * ch]
    if masks:
        split_halves(total, spot[1], kept, sent)


def input_grads(spot, own, near, far, *rest, masks):
    if masks:
        lists, rest = rest[:4], rest[4:]
        (padded, pairs), rest = rest[-2:], rest[:-2]
        kept_one, kept_two, out, one_on, two_on = rest
        one_on[...] = kept_one[...]
        two_on[...] = kept_two[...]
        mine, theirs = both_columns(lists)
        weights = placed_weights(spot, masks, mine, theirs, pairs)
    else:
        full, out, padded = rest
        weights = plain_weights(full)
    fill_padded(spot, padded, own, near, far)

    def finish(x, y, value):
        out[x, y] = value.astype(bf16)

    data_layers(padded, weights, finish, range(out.shape[0]))


def stack(*refs, counts):
    ins, outs = refs[: sum(counts)], refs[sum(counts) :]
    for count, out in zip(counts, outs):
        at = 0
        for part in ins[:count]:
            if len(part.shape) < len(out.shape):
                out[at] = part[...]
                at += 1
            else:
                out[at : at + part.shape[0]] = part[...]
                at += part.shape[0]
        ins = ins[count:]


def halve(spot, kept, got, kept_next, sent_next, *, bit):
    side = spot[bit - 1]
    for k in range(kept_next.shape[0]):
        mine, other = 2 * k + side, 2 * k + 1 - side
        kept_next[k] = kept[mine] + got[mine].astype(f32)
        sent_next[k] = (kept[other] + got[other].astype(f32)).astype(bf16)


def halve_and_pass(spot, kept, got, near, far, kept_next, sent_next, near_on, far_on, *, bit):
    halve(spot, kept, got, kept_next, sent_next, bit=bit)
    near_on[...] = near[...]
    far_on[...] = far[...]


def last_sums(kept_a, got_a, kept_b, got_b, out_a, out_b):
    out_a[...] = kept_a[0] + got_a[0].astype(f32)
    out_b[...] = kept_b[0] + got_b[0].astype(f32)


def call(body, n_smem, args, outs, scratch=(), after=(), us=0.2):
    args = args[n_smem:]
    first, many = len(args), len(after)

    def run(*refs):
        refs = refs[:first] + refs[first + many :]
        if n_smem:
            me = lax.axis_index("gx")
            body([me] + [(me >> k) & 1 for k in range(4)], *refs)
        else:
            body(*refs)

    return pl.pallas_call(
        run,
        in_specs=[vmem] * first + [anywhere] * many,
        out_specs=[vmem] * len(outs),
        out_shape=[jax.ShapeDtypeStruct(s, d) for s, d in outs],
        scratch_shapes=[pltpu.VMEM(s, d) for s, d in scratch],
        cost_estimate=pl.CostEstimate(flops=int(us * 1e9), bytes_accessed=int(us * 3e6), transcendentals=0),
        compiler_params=pltpu.CompilerParams(vmem_limit_bytes=vmem_bytes),
    )(*args, *after)


def on_device(grad_out, inputs, pre_first, pre_second, filter_first, filter_second):
    shape = grad_out.shape
    nx, ny, nz, ch = shape
    n = lax.axis_size("gx")
    me = lax.axis_index("gx")
    rows = filter_first.shape[0]
    taps = n * rows // ch
    scale = 1.0 / math.sqrt(nx * n * ny * nz)
    spot = None
    fast = rows % 8 == 0 and n == 1 << 4
    masks_two = (0, 8, 4, 12, 2, 10, 6, 14) if fast else ()
    masks_one = (0, 2, 8, 10, 4, 6, 12, 14) if fast else ()
    layer = (1,) + shape[1:]
    block = (rows, ch)
    wide = ((nx + 2, ny + 2, nz, ch), bf16)
    cells = nx * ny * nz
    total = ((taps * ch, ch), f32)

    def swap(array, mask):
        return lax.ppermute(array, "gx", [(i, i ^ mask) for i in range(n)])

    def swap_far(array):
        ahead = [(i, i + 1) for i in range(1, n - 1, 2)]
        return lax.ppermute(array, "gx", ahead + [(b, a) for a, b in ahead])

    def blocks(count, dtype=bf16):
        return ((count,) + block, dtype)

    def stacked(groups, sizes, after, us=0.2):
        parts = [part for group in groups for part in group]
        body = functools.partial(stack, counts=[len(group) for group in groups])
        return call(body, 0, parts, [blocks(size) for size in sizes], after=after, us=us)

    terms = [blocks(n // 2, f32), blocks(n // 2)] if fast else [total]
    work = [total, ((n // 2, 2 * rows, ch), bf16)] if fast else []

    grad_two = (grad_out.astype(f32) * slope_of(pre_second.astype(f32))).astype(bf16)
    near, far = call(send_edges, 1, (spot, grad_two), [(layer, bf16), (layer, bf16)], us=20)
    after = (near,)
    far = swap_far(far)
    near = swap(near, 1)
    if fast:
        pair, pair_first = stacked(
            [(filter_second, swap(filter_second, 8)), (filter_first, swap(filter_first, 2))], (2, 2), after
        )
        after = (pair,)
    turned, turned_own, slope = call(
        prepare,
        1,
        (spot, pre_first, inputs),
        [((3 * ch, cells), bf16), ((nx, ny, ch, nz), bf16), (shape, f32)],
        after=after,
        us=4,
    )
    (grads_wide,) = call(widen, 1, (spot, grad_two, near, far), [wide], after=(turned,), us=20)
    sides = ((2, ny, ch, nz), bf16)
    if fast:
        column, near_in, far_in = call(
            stack_and_edges,
            1,
            (spot, pair, swap(pair, 4), inputs),
            [blocks(4), (layer, bf16), (layer, bf16)],
            after=(grads_wide,),
            us=20,
        )
        after = (column,)
    else:
        near_in, far_in = call(send_edges, 1, (spot, inputs), [(layer, bf16), (layer, bf16)])
        after = ()
    terms_two = call(
        functools.partial(second_filter, scale=scale, fast=fast),
        1,
        (spot, grads_wide, turned),
        terms,
        work[:1],
        after=after,
        us=2,
    )
    near_in, far_in = swap(near_in, 1), swap_far(far_in)
    if fast:
        across = swap(column, 2)
        after = (across,)
    else:
        full_second = (lax.all_gather(filter_second, "gx", axis=0, tiled=True),)
        after = ()
    (turned_sides,) = call(turn_sides, 1, (spot, near_in, far_in), [sides], after=after, us=20)
    if fast:
        kept_two, sent_two = call(
            functools.partial(halve, bit=3),
            1,
            (spot, terms_two[0], swap(terms_two[1], 1)),
            [blocks(4, f32), blocks(4)],
            after=(turned_sides,),
        )
        (column_first,) = stacked([(pair_first, swap(pair_first, 8))], (4,), (kept_two,))
        after = (column_first,)
        full_second = (column, across, swap(column, 1), swap(across, 1))

    *terms_one, grad_one, near_one, far_one = call(
        functools.partial(first_filter, scale=scale, masks=masks_two),
        1,
        (spot, slope, grads_wide, turned_own, turned_sides, *full_second),
        terms + [(shape, bf16), (layer, bf16), (layer, bf16)],
        [((cells, 3 * ch), bf16), ((len(planes) * ch, cells), bf16)] + work,
        after=after,
        us=8,
    )

    def finish(near, far, full, sums=()):
        sizes = [blocks(1, f32)] * len(sums)
        return call(
            functools.partial(input_grads, masks=masks_one),
            1,
            (spot, grad_one, swap(near, 1), swap_far(far), *full, *sums),
            [(shape, bf16)] + sizes,
            [wide] + work[1:],
            us=5,
        )

    if fast:

        def step(kept, sent, bit, mask, count, after, us=0.2):
            return call(
                functools.partial(halve, bit=bit),
                1,
                (spot, kept, swap(sent, mask)),
                [blocks(count, f32), blocks(count)],
                after=after,
                us=us,
            )

        kept_two, sent_two = step(kept_two, sent_two, 4, 2, 2, (grad_one,), 20)
        kept_one, sent_one = step(*terms_one, 3, 1, 4, (kept_two,))
        mine = (column_first, swap(column_first, 4))
        full_first = (*mine, *(swap(m, 1) for m in mine))
        kept_two, sent_two = step(kept_two, sent_two, 5, 4, 1, (kept_one, *full_first), 0.2)
        got_two = swap(sent_two, 8)
        kept_one, sent_one, near_one, far_one = call(
            functools.partial(halve_and_pass, bit=4),
            1,
            (spot, kept_one, swap(sent_one, 2), near_one, far_one),
            [blocks(2, f32), blocks(2), (layer, bf16), (layer, bf16)],
            after=(kept_two,),
            us=20,
        )
        kept_one, sent_one = step(kept_one, sent_one, 5, 4, 1, (), 1.5)
        grad_in, kept_one, kept_two = finish(near_one, far_one, full_first, (kept_one, kept_two))
        owned_two, owned_one = call(
            last_sums, 0, (kept_two, got_two, kept_one, swap(sent_one, 8)), [(block, f32)] * 2
        )
    else:
        (grad_in,) = finish(near_one, far_one, (lax.all_gather(filter_first, "gx", axis=0, tiled=True),))
        owned_two, owned_one = (
            lax.psum_scatter(t[0], "gx", scatter_dimension=0, tiled=True) for t in (terms_two, terms_one)
        )
    return (grad_in, owned_one, owned_two)


def solution(mesh):
    whole = P(("groups", "gx"), None, None, None)
    return jax.shard_map(
        on_device,
        mesh=mesh,
        in_specs=(whole, whole, whole, whole, P("gx", None), P("gx", None)),
        out_specs=(whole, P("gx", "groups"), P("gx", "groups")),
        check_vma=False,
    )
```

```python
import functools
import math

import jax
import jax.numpy as jnp
from jax import lax
from jax.experimental import pallas as pl
from jax.experimental.pallas import tpu as pltpu
from jax.sharding import PartitionSpec as P

inv_root_two = 0.7071067811865476
inv_root_twopi = 0.3989422804014327
shifts = (-1, 0, 1)
planes = tuple((a, b) for a in shifts for b in shifts)
bf16, f32 = jnp.bfloat16, jnp.float32
vmem = pl.BlockSpec(memory_space=pltpu.VMEM)
anywhere = pl.BlockSpec(memory_space=pl.ANY)
vmem_bytes = 14 * 1024 * 1024


def cdf_of(value):
    return 0.5 * (1.0 + lax.erf(value * inv_root_two))


def slope_of(value):
    return cdf_of(value) + value * jnp.exp(-0.5 * value * value) * inv_root_twopi


def value_of(value):
    return value * cdf_of(value)


def shift_rows(block, c):
    rows = block.shape[0]
    if c == 0:
        return block
    place = lax.broadcasted_iota(jnp.int32, block.shape, 0)
    edge = 0 if c == 1 else rows - 1
    return jnp.where(place == edge, 0.0, pltpu.roll(block, c % rows, 0))


def zero_sides(ref):
    layers, wide = ref.shape[:2]
    blank = jnp.zeros(ref.shape[2:], ref.dtype)
    for x in range(layers):
        ref[x, 0] = blank
        ref[x, wide - 1] = blank


def near_edge(spot, last):
    return last * (1 - spot[1])


def send_edges(spot, own, near, far):
    last = own.shape[0] - 1
    at = near_edge(spot, last)
    near[0] = own[at]
    far[0] = own[last - at]


def filter_terms(turned, padded, emit, scale):
    nx, ny = padded.shape[0] - 2, padded.shape[1] - 2
    nz, ch = padded.shape[2:]
    rows = nx * ny * nz

    def piece(a, b):
        return padded[1 - a : 1 - a + nx, 1 - b : 1 - b + ny].reshape(rows, ch)

    for i in range(0, len(planes), 2):
        pair = planes[i : i + 2]
        right = jnp.concatenate([piece(a, b) for a, b in pair], axis=1)
        part = jnp.dot(turned[...], right, preferred_element_type=f32) * scale
        for j in range(len(pair)):
            emit(i + j, part[:, j * ch : (j + 1) * ch])


def prepare(spot, pre_first, inputs, turned, turned_own, slope):
    nx, ny, nz, ch = pre_first.shape
    for x in range(nx):
        for y in range(ny):
            value = pre_first[x, y].astype(f32)
            slope[x, y] = slope_of(value)
            block = value_of(value).astype(bf16).astype(f32)
            at = (x * ny + y) * nz
            for k, c in enumerate(shifts):
                turned[k * ch : (k + 1) * ch, at : at + nz] = shift_rows(block, -c).T.astype(bf16)
            turned_own[x, y] = inputs[x, y].astype(f32).T.astype(bf16)


def stack_turned(stacked, turned_own, turned_sides):
    nx, ny, ch, nz = turned_own.shape
    blank = jnp.zeros((ch, nz), bf16)
    for i, (a, b) in enumerate(planes):
        for x in range(nx):
            for y in range(ny):
                if 0 <= y + b < ny:
                    inside = 0 <= x + a < nx
                    block = turned_own[x + a, y + b] if inside else turned_sides[int(x + a == nx), y + b]
                else:
                    block = blank
                at = (x * ny + y) * nz
                stacked[i * ch : (i + 1) * ch, at : at + nz] = block


def data_layers(padded, weights, finish, out_x):
    ny = padded.shape[1] - 2
    nz, ch = padded.shape[2:]
    rows = ny * nz
    for x in out_x:
        total = None
        for i in range(0, len(planes), 2):
            pair = planes[i : i + 2]
            left = jnp.concatenate(
                [padded[1 + x - a, 1 - b : 1 - b + ny].reshape(rows, ch) for a, b in pair], axis=1
            )
            right = jnp.concatenate([weights(i + j) for j in range(len(pair))], axis=1)
            part = lax.dot_general(left, right, (((1,), (1,)), ((), ())), preferred_element_type=f32)
            total = part if total is None else total + part
        for y in range(ny):
            block = total[y * nz : (y + 1) * nz]
            value = sum(shift_rows(block[:, k * ch : (k + 1) * ch], c) for k, c in enumerate(shifts))
            finish(x, y, value)


def fill_padded(spot, padded, own, near, far):
    nx, ny = own.shape[:2]
    zero_sides(padded)
    padded[1 : 1 + nx, 1 : 1 + ny] = own[...]
    at = near_edge(spot, nx + 1)
    padded[at, 1 : 1 + ny] = near[0]
    padded[nx + 1 - at, 1 : 1 + ny] = far[0]


def widen(spot, own, near, far, padded):
    fill_padded(spot, padded, own, near, far)


def split_halves(total, side, kept, sent):
    half, rows = kept.shape[:2]
    for k in range(half):
        kept[k] = total[pl.ds(pl.multiple_of((2 * k + side) * rows, 8), rows)]
        sent[k] = total[pl.ds(pl.multiple_of((2 * k + 1 - side) * rows, 8), rows)].astype(bf16)


def plain_weights(full):
    ch = full.shape[1]
    return lambda plane: full[plane * 3 * ch : (plane + 1) * 3 * ch]


def placed_weights(spot, masks, mine, theirs, pairs):
    even = spot[1] == 0
    for mask, first, second in zip(masks, mine, theirs):
        one, two = first[...].astype(f32), second[...].astype(f32)
        both = jnp.concatenate([jnp.where(even, one, two), jnp.where(even, two, one)], axis=0)
        pairs[lax.bitwise_xor(spot[0] >> 1, mask // 2)] = both.astype(bf16)
    wide, ch = pairs.shape[1:]

    def weights(plane):
        at, end = plane * 3 * ch, (plane + 1) * 3 * ch
        pieces = []
        while at < end:
            stop = min(end, (at // wide + 1) * wide)
            pieces.append(pairs[at // wide, at % wide : at % wide + stop - at])
            at = stop
        return jnp.concatenate(pieces, axis=0) if len(pieces) > 1 else pieces[0]

    return weights


def second_filter(spot, padded, turned, *rest, scale, fast):
    total, outs = (rest[-1], rest[:2]) if fast else (rest[0], ())

    def emit(plane, part):
        ch = part.shape[1]
        total[plane * 3 * ch : (plane + 1) * 3 * ch] = part

    filter_terms(turned, padded, emit, scale)
    if fast:
        split_halves(total, spot[1], *outs)

def turn_sides(spot, near, far, turned_sides):
    high = near_edge(spot, 1)
    for y in range(near.shape[1]):
        turned_sides[high, y] = near[0, y].astype(f32).T.astype(bf16)
        turned_sides[1 - high, y] = far[0, y].astype(f32).T.astype(bf16)


def stack_and_edges(spot, pair, other, inputs, column, near, far):
    count = pair.shape[0]
    column[0:count] = pair[...]
    column[count:] = other[...]
    send_edges(spot, inputs, near, far)


def both_columns(lists):
    split = [[ref.at[k] for k in range(ref.shape[0])] for ref in lists]
    return split[0] + split[1], split[2] + split[3]


def first_filter(spot, slope, padded, turned_own, turned_sides, *rest, scale, masks):
    nx, ny, nz, ch = slope.shape
    if masks:
        kept, sent, grads, near_one, far_one, moved, stacked, total, pairs = rest[4:]
        mine, theirs = both_columns(rest[:4])
        weights = placed_weights(spot, masks, mine, theirs, pairs)
    else:
        full, total, grads, near_one, far_one, moved, stacked = rest
        weights = plain_weights(full)

    def finish(x, y, value):
        value = (value * slope[x, y]).astype(bf16)
        grads[x, y] = value
        value = value.astype(f32)
        at = (x * ny + y) * nz
        for k, c in enumerate(shifts):
            moved[at : at + nz, k * ch : (k + 1) * ch] = shift_rows(value, c).astype(bf16)

    data_layers(padded, weights, finish, range(nx))
    send_edges(spot, grads, near_one, far_one)
    stack_turned(stacked, turned_own, turned_sides)
    part = jnp.dot(stacked[...], moved[...], preferred_element_type=f32) * scale
    for i in range(len(planes)):
        for k in range(len(shifts)):
            at = (i * len(shifts) + k) * ch
            total[at : at + ch] = part[i * ch : (i + 1) * ch, k * ch : (k + 1) * ch]
    if masks:
        split_halves(total, spot[1], kept, sent)


def input_grads(spot, own, near, far, *rest, masks):
    if masks:
        lists, rest = rest[:4], rest[4:]
        (padded, pairs), rest = rest[-2:], rest[:-2]
        kept_one, kept_two, out, one_on, two_on = rest
        one_on[...] = kept_one[...]
        two_on[...] = kept_two[...]
        mine, theirs = both_columns(lists)
        weights = placed_weights(spot, masks, mine, theirs, pairs)
    else:
        full, out, padded = rest
        weights = plain_weights(full)
    fill_padded(spot, padded, own, near, far)

    def finish(x, y, value):
        out[x, y] = value.astype(bf16)

    data_layers(padded, weights, finish, range(out.shape[0]))


def stack(*refs, counts):
    ins, outs = refs[: sum(counts)], refs[sum(counts) :]
    for count, out in zip(counts, outs):
        at = 0
        for part in ins[:count]:
            if len(part.shape) < len(out.shape):
                out[at] = part[...]
                at += 1
            else:
                out[at : at + part.shape[0]] = part[...]
                at += part.shape[0]
        ins = ins[count:]


def halve(spot, kept, got, kept_next, sent_next, *, bit):
    side = spot[bit - 1]
    for k in range(kept_next.shape[0]):
        mine, other = 2 * k + side, 2 * k + 1 - side
        kept_next[k] = kept[mine] + got[mine].astype(f32)
        sent_next[k] = (kept[other] + got[other].astype(f32)).astype(bf16)


def halve_and_pass(spot, kept, got, near, far, kept_next, sent_next, near_on, far_on, *, bit):
    halve(spot, kept, got, kept_next, sent_next, bit=bit)
    near_on[...] = near[...]
    far_on[...] = far[...]


def last_sums(kept_a, got_a, kept_b, got_b, out_a, out_b):
    out_a[...] = kept_a[0] + got_a[0].astype(f32)
    out_b[...] = kept_b[0] + got_b[0].astype(f32)


def call(body, n_smem, args, outs, scratch=(), after=(), us=0.2):
    args = args[n_smem:]
    first, many = len(args), len(after)

    def run(*refs):
        refs = refs[:first] + refs[first + many :]
        if n_smem:
            me = lax.axis_index("gx")
            body([me] + [(me >> k) & 1 for k in range(4)], *refs)
        else:
            body(*refs)

    return pl.pallas_call(
        run,
        in_specs=[vmem] * first + [anywhere] * many,
        out_specs=[vmem] * len(outs),
        out_shape=[jax.ShapeDtypeStruct(s, d) for s, d in outs],
        scratch_shapes=[pltpu.VMEM(s, d) for s, d in scratch],
        cost_estimate=pl.CostEstimate(flops=int(us * 1e9), bytes_accessed=int(us * 3e6), transcendentals=0),
        compiler_params=pltpu.CompilerParams(vmem_limit_bytes=vmem_bytes),
    )(*args, *after)


def on_device(grad_out, inputs, pre_first, pre_second, filter_first, filter_second):
    shape = grad_out.shape
    nx, ny, nz, ch = shape
    n = lax.axis_size("gx")
    me = lax.axis_index("gx")
    rows = filter_first.shape[0]
    taps = n * rows // ch
    scale = 1.0 / math.sqrt(nx * n * ny * nz)
    spot = None
    fast = rows % 8 == 0 and n == 1 << 4
    masks_two = (0, 8, 4, 12, 2, 10, 6, 14) if fast else ()
    masks_one = (0, 2, 8, 10, 4, 6, 12, 14) if fast else ()
    layer = (1,) + shape[1:]
    block = (rows, ch)
    wide = ((nx + 2, ny + 2, nz, ch), bf16)
    cells = nx * ny * nz
    total = ((taps * ch, ch), f32)

    def swap(array, mask):
        return lax.ppermute(array, "gx", [(i, i ^ mask) for i in range(n)])

    def swap_far(array):
        ahead = [(i, i + 1) for i in range(1, n - 1, 2)]
        return lax.ppermute(array, "gx", ahead + [(b, a) for a, b in ahead])

    def blocks(count, dtype=bf16):
        return ((count,) + block, dtype)

    def stacked(groups, sizes, after, us=0.2):
        parts = [part for group in groups for part in group]
        body = functools.partial(stack, counts=[len(group) for group in groups])
        return call(body, 0, parts, [blocks(size) for size in sizes], after=after, us=us)

    terms = [blocks(n // 2, f32), blocks(n // 2)] if fast else [total]
    work = [total, ((n // 2, 2 * rows, ch), bf16)] if fast else []

    grad_two = (grad_out.astype(f32) * slope_of(pre_second.astype(f32))).astype(bf16)
    near, far = call(send_edges, 1, (spot, grad_two), [(layer, bf16), (layer, bf16)], us=20)
    after = (near,)
    far = swap_far(far)
    near = swap(near, 1)
    if fast:
        pair, pair_first = stacked(
            [(filter_second, swap(filter_second, 8)), (filter_first, swap(filter_first, 2))], (2, 2), after
        )
        after = (pair,)
    turned, turned_own, slope = call(
        prepare,
        1,
        (spot, pre_first, inputs),
        [((3 * ch, cells), bf16), ((nx, ny, ch, nz), bf16), (shape, f32)],
        after=after,
        us=4,
    )
    (grads_wide,) = call(widen, 1, (spot, grad_two, near, far), [wide], after=(turned,), us=20)
    sides = ((2, ny, ch, nz), bf16)
    if fast:
        column, near_in, far_in = call(
            stack_and_edges,
            1,
            (spot, pair, swap(pair, 4), inputs),
            [blocks(4), (layer, bf16), (layer, bf16)],
            after=(grads_wide,),
            us=20,
        )
        after = (column,)
    else:
        near_in, far_in = call(send_edges, 1, (spot, inputs), [(layer, bf16), (layer, bf16)])
        after = ()
    terms_two = call(
        functools.partial(second_filter, scale=scale, fast=fast),
        1,
        (spot, grads_wide, turned),
        terms,
        work[:1],
        after=after,
        us=2,
    )
    near_in, far_in = swap(near_in, 1), swap_far(far_in)
    if fast:
        across = swap(column, 2)
        after = (across,)
    else:
        full_second = (lax.all_gather(filter_second, "gx", axis=0, tiled=True),)
        after = ()
    (turned_sides,) = call(turn_sides, 1, (spot, near_in, far_in), [sides], after=after, us=20)
    if fast:
        kept_two, sent_two = call(
            functools.partial(halve, bit=3),
            1,
            (spot, terms_two[0], swap(terms_two[1], 1)),
            [blocks(4, f32), blocks(4)],
            after=(turned_sides,),
        )
        (column_first,) = stacked([(pair_first, swap(pair_first, 8))], (4,), (kept_two,))
        after = (column_first,)
        full_second = (column, across, swap(column, 1), swap(across, 1))

    *terms_one, grad_one, near_one, far_one = call(
        functools.partial(first_filter, scale=scale, masks=masks_two),
        1,
        (spot, slope, grads_wide, turned_own, turned_sides, *full_second),
        terms + [(shape, bf16), (layer, bf16), (layer, bf16)],
        [((cells, 3 * ch), bf16), ((len(planes) * ch, cells), bf16)] + work,
        after=after,
        us=8,
    )

    def finish(near, far, full, sums=()):
        sizes = [blocks(1, f32)] * len(sums)
        return call(
            functools.partial(input_grads, masks=masks_one),
            1,
            (spot, grad_one, swap(near, 1), swap_far(far), *full, *sums),
            [(shape, bf16)] + sizes,
            [wide] + work[1:],
            us=5,
        )

    if fast:

        def step(kept, sent, bit, mask, count, after, us=0.2):
            return call(
                functools.partial(halve, bit=bit),
                1,
                (spot, kept, swap(sent, mask)),
                [blocks(count, f32), blocks(count)],
                after=after,
                us=us,
            )

        kept_two, sent_two = step(kept_two, sent_two, 4, 2, 2, (grad_one,), 3)
        kept_one, sent_one = step(*terms_one, 3, 1, 4, (kept_two,))
        mine = (column_first, swap(column_first, 4))
        full_first = (*mine, *(swap(m, 1) for m in mine))
        kept_two, sent_two = step(kept_two, sent_two, 5, 4, 1, (kept_one, *full_first), 0.2)
        got_two = swap(sent_two, 8)
        kept_one, sent_one, near_one, far_one = call(
            functools.partial(halve_and_pass, bit=4),
            1,
            (spot, kept_one, swap(sent_one, 2), near_one, far_one),
            [blocks(2, f32), blocks(2), (layer, bf16), (layer, bf16)],
            after=(kept_two,),
            us=20,
        )
        kept_one, sent_one = step(kept_one, sent_one, 5, 4, 1, (), 1.5)
        grad_in, kept_one, kept_two = finish(near_one, far_one, full_first, (kept_one, kept_two))
        owned_two, owned_one = call(
            last_sums, 0, (kept_two, got_two, kept_one, swap(sent_one, 8)), [(block, f32)] * 2
        )
    else:
        (grad_in,) = finish(near_one, far_one, (lax.all_gather(filter_first, "gx", axis=0, tiled=True),))
        owned_two, owned_one = (
            lax.psum_scatter(t[0], "gx", scatter_dimension=0, tiled=True) for t in (terms_two, terms_one)
        )
    return (grad_in, owned_one, owned_two)


def solution(mesh):
    whole = P(("groups", "gx"), None, None, None)
    return jax.shard_map(
        on_device,
        mesh=mesh,
        in_specs=(whole, whole, whole, whole, P("gx", None), P("gx", None)),
        out_specs=(whole, P("gx", "groups"), P("gx", "groups")),
        check_vma=False,
    )
```
